32 devices in a mesh: nodes: 8 (over z, x), mp: 4 (over y, core).
Axes of the slice: x: 2, y: 2, z: 4, core: 2. Of those that a mesh axis runs over, the one named last changes fastest.
Arguments:
- tokens: bfloat16 [256, 64, 768], P('nodes'), may hold values from -32 to 32
- w_query: bfloat16 [768, 768], P('mp'), may hold values from -0.5 to 0.5
- w_key: bfloat16 [768, 768], P('mp'), may hold values from -0.5 to 0.5
- w_value: bfloat16 [768, 768], P('mp'), may hold values from -0.21875 to 0.21875
- grad_out: bfloat16 [256, 12, 4096], P('nodes', 'mp'), may hold values from -6 to 6
- owned_cls: bfloat16 [768, 16384], P('mp', 'nodes'), may hold values from -24 to 24
- send_rows: int32 [8, 8, 256], P('nodes'), may hold values from 0 to 2047
- neigh_slot: int32 [256, 2, 32], P('nodes'), may hold values from 0 to 2047
- neigh_count: int32 [256, 2], P('nodes'), may hold values from 1 to 32
Outputs:
- context: bfloat16 [256, 12, 4096], P('nodes', 'mp')
- grad_query: float32 [768, 768], P('mp')
- grad_key: float32 [768, 768], P('mp')
- grad_value: float32 [768, 768], P('mp')
- grad_cls: float32 [768, 16384], P('mp', 'nodes')
The draws below stay inside these ranges and needn't reach their ends.
Inputs may be any that keep to these rules, and one draw needn't show every extreme that they name: send_rows[o, r, :] are rows of owner o's own block; rows may repeat. `neigh_slot`: entries with k >= neigh_count[c, t] are not used.
All inputs are finite; a program needn't handle non-finite values.
Results may differ from the reference program's by a relative error of at most 0.012.
The reference program's roundings to bfloat16 on the way (of `fetched`, `virtual`, `key_input`, `probs_low`, `value_grads` and `score_grads`) count: a program that leaves them out, or rounds other values in their place, can miss the bound.
Values may be sent and summed in bfloat16 or wider, within the bound.
A program may use at most 128 MiB of HBM per device.

```python
import math
import jax
import jax.numpy as jnp
import numpy as np
from jax import lax

D = 768
HEADS = 12
HD = 64
L = 64
NT = 2
K = 32
CEN_DEV = 32
OWN_DEV = 2048
CENTRES = 256
OWNED = 16384
OWNERS = 8
REQ_DEV = 2048
CAP = 256
N_NODES = 8


def shared_query(key):
    return jax.random.normal(jax.random.fold_in(key, 7001), (D, D), jnp.float32) / math.sqrt(D)


def draw_w_query(key, part):
    return jnp.clip(shared_query(key), -0.5, 0.5).astype(jnp.bfloat16)


def draw_w_key(key, part):
    fresh_noise = jax.random.normal(jax.random.fold_in(key, 7002), (D, D), jnp.float32) / math.sqrt(D)
    mixed = fresh_noise
    return jnp.clip(mixed, -0.5, 0.5).astype(jnp.bfloat16)


def draw_tokens(key, part):
    normal_draw = jax.random.normal(jax.random.fold_in(key, 7010), (CENTRES, L, D), jnp.float32)
    return jnp.clip(normal_draw, -32.0, 32.0).astype(jnp.bfloat16)


def with_ends(array, stream_key, smallest, top_value):
    longest = array.shape.index(max(array.shape))
    spots = []
    for shift in (0, 1):
        where = [jax.random.randint(jax.random.fold_in(stream_key, axis), (), 0, length) for axis, length in enumerate(array.shape)]
        where[longest] = (where[longest] + shift) % array.shape[longest]
        spots.append(tuple(where))
    return array.at[spots[0]].set(smallest).at[spots[1]].set(top_value)


def levels(own_key, extent, shards, smallest, largest):
    gain, own = 1.0, jax.random.fold_in(own_key, 6)
    for dim, parts in shards:
        steps = jnp.exp(jax.random.uniform(jax.random.fold_in(own, dim), (parts,), jnp.float32, smallest / len(shards), largest / len(shards)))
        gain = gain * jnp.repeat(steps, extent[dim] // parts).reshape([-1 if axis == dim else 1 for axis in range(len(extent))])
    return gain


def rank_table(number_of, skew):
    loads = [(1 << 20) // math.isqrt(rank ** skew) + 1 for rank in range(1, number_of + 1)]
    spread = 1 + sum(loads) // (1 << 30)
    return np.cumsum(np.array([max(1, weight // spread) for weight in loads]))


def skewed_ids(key, dims, count, slope):
    table = rank_table(count, slope)
    ticket = jax.random.randint(jax.random.fold_in(key, 1), dims, 0, int(table[count - 1]))
    standing = jnp.searchsorted(jnp.asarray(table, jnp.int32), ticket, side="right")
    return jax.random.permutation(jax.random.fold_in(key, 2), count)[standing].astype(jnp.int32)


def scatter_about(key, extent, spread, reach, split=(), kind=jnp.bfloat16):
    drawn = spread * jax.random.normal(key, extent, jnp.float32)
    if split:
        drawn = drawn * levels(key, extent, split, -0.22, 0.18)
    return jnp.clip(drawn, -reach, reach).astype(kind)


def setup_inputs(seed: int = 0) -> dict:
    key_of = jax.random.split(jax.random.key(seed), 10)
    tokens = draw_tokens(jax.random.fold_in(key_of[9], 71), 0)
    w_query = draw_w_query(jax.random.fold_in(key_of[9], 71), 0)
    w_key = draw_w_key(jax.random.fold_in(key_of[9], 71), 0)
    w_value = scatter_about(key_of[3], (D, D), D ** -0.5, 0.21875, ((0, 4),))
    grad_out = scatter_about(key_of[4], (CENTRES, HEADS, L * HD), 1.0, 6.0, ((0, 8), (1, 4)))
    owned_cls = scatter_about(key_of[5], (D, OWNED), 4.0, 24.0, ((0, 4), (1, 8)))
    send_rows = with_ends(skewed_ids(key_of[6], (OWNERS, OWNERS, CAP), OWN_DEV, 2), jax.random.fold_in(key_of[6], 3), 0, OWN_DEV - 1).astype(jnp.int32)
    neigh_slot = with_ends(jax.random.randint(key_of[7], (CENTRES, NT, K), 0, REQ_DEV), jax.random.fold_in(key_of[7], 1), 0, REQ_DEV - 1).astype(jnp.int32)
    neigh_count = with_ends(jax.random.randint(key_of[8], (CENTRES, NT), 1, K + 1), jax.random.fold_in(key_of[8], 1), 1, K).astype(jnp.int32)
    return dict(tokens=tokens, w_query=w_query, w_key=w_key, w_value=w_value, grad_out=grad_out, owned_cls=owned_cls, send_rows=send_rows, neigh_slot=neigh_slot, neigh_count=neigh_count)


def attend(text_tokens, virtual, query_weight, key_weight, value_weight, grad_text):
    centres = text_tokens.shape[0]
    key_input = jnp.concatenate([virtual, text_tokens], axis=1)
    flat_tokens = text_tokens.reshape(-1, D)
    flat_keys = key_input.reshape(-1, D)
    queries = jnp.dot(flat_tokens, query_weight, preferred_element_type=jnp.float32).astype(jnp.bfloat16).reshape(centres, L, HEADS, HD)
    keys = jnp.dot(flat_keys, key_weight, preferred_element_type=jnp.float32).astype(jnp.bfloat16).reshape(centres, NT + L, HEADS, HD)
    values = jnp.dot(flat_keys, value_weight, preferred_element_type=jnp.float32).astype(jnp.bfloat16).reshape(centres, NT + L, HEADS, HD)
    score_scale = 1.0 / math.sqrt(HD)
    scores = jnp.einsum('clhe,cmhe->chlm', queries.astype(jnp.float32), keys.astype(jnp.float32)) * score_scale
    attn_probs = jax.nn.softmax(scores, axis=-1)
    probs_low = attn_probs.astype(jnp.bfloat16)
    context = jnp.einsum('chlm,cmhe->clhe', probs_low.astype(jnp.float32), values.astype(jnp.float32)).astype(jnp.bfloat16)
    grad_heads = grad_text.reshape(centres, L, HEADS, HD).astype(jnp.float32)
    prob_grads = jnp.einsum('clhe,cmhe->chlm', grad_heads, values.astype(jnp.float32))
    value_grads = jnp.einsum('chlm,clhe->cmhe', probs_low.astype(jnp.float32), grad_heads).astype(jnp.bfloat16)
    score_grads = attn_probs * (prob_grads - lax.optimization_barrier(jnp.sum(prob_grads * attn_probs, axis=-1, keepdims=True))) * score_scale
    score_low = score_grads.astype(jnp.bfloat16).astype(jnp.float32)
    query_grads = jnp.einsum('chlm,cmhe->clhe', score_low, keys.astype(jnp.float32)).astype(jnp.bfloat16)
    key_grads = jnp.einsum('chlm,clhe->cmhe', score_low, queries.astype(jnp.float32)).astype(jnp.bfloat16)
    part_query = jnp.dot(flat_tokens.T, query_grads.reshape(-1, D), preferred_element_type=jnp.float32)
    part_key = jnp.dot(flat_keys.T, key_grads.reshape(-1, D), preferred_element_type=jnp.float32)
    part_value = jnp.dot(flat_keys.T, value_grads.reshape(-1, D), preferred_element_type=jnp.float32)
    virtual_key = key_grads[:, :NT].reshape(-1, D)
    virtual_value = value_grads[:, :NT].reshape(-1, D)
    virtual_grads = jnp.dot(virtual_key, key_weight.T, preferred_element_type=jnp.float32) + jnp.dot(virtual_value, value_weight.T, preferred_element_type=jnp.float32)
    return (context, part_query, part_key, part_value, virtual_grads.reshape(centres, NT, D))

def reference(tokens, w_query, w_key, w_value, grad_out, owned_cls, send_rows, neigh_slot, neigh_count):
    query_weight = w_query.T
    key_weight = w_key.T
    value_weight = w_value.T
    owned_blocks = owned_cls.T.reshape(N_NODES, OWN_DEV, D)
    token_blocks = tokens.reshape(N_NODES, CEN_DEV, L, D)
    grad_text = grad_out.reshape(CENTRES, HEADS, L, HD).transpose(0, 2, 1, 3).reshape(CENTRES, L, D)
    grad_blocks = grad_text.reshape(N_NODES, CEN_DEV, L, D)
    slot_blocks = neigh_slot.reshape(N_NODES, CEN_DEV, NT, K)
    count_blocks = neigh_count.reshape(N_NODES, CEN_DEV, NT)
    owner_ids = jnp.arange(N_NODES, dtype=jnp.int32)[:, None]
    positions = jnp.arange(K, dtype=jnp.int32)

    def per_device(totals, device_index):
        total_query, total_key, total_value, cls_total = totals
        rows_sent = send_rows[:, device_index, :]
        fetched = owned_blocks[owner_ids, rows_sent].reshape(REQ_DEV, D)
        slots = slot_blocks[device_index]
        counts = count_blocks[device_index]
        live_mask = (positions[None, None, :] < counts[:, :, None]).astype(jnp.float32)
        picked = fetched[slots].astype(jnp.float32)
        denominator = counts.astype(jnp.float32)
        virtual = (lax.optimization_barrier(jnp.sum(live_mask[..., None] * picked, axis=2)) / denominator[..., None]).astype(jnp.bfloat16)
        context, part_query, part_key, part_value, virtual_grads = attend(token_blocks[device_index], virtual, query_weight, key_weight, value_weight, grad_blocks[device_index])
        shared_grad = virtual_grads / denominator[..., None]
        slot_terms = (live_mask[..., None] * shared_grad[:, :, None, :]).reshape(-1, D)
        slot_grads = jax.ops.segment_sum(slot_terms, slots.reshape(-1), num_segments=REQ_DEV).reshape(N_NODES, CAP, D)
        cls_total = cls_total.at[owner_ids, rows_sent].add(slot_grads)
        return ((total_query + part_query, total_key + part_key, total_value + part_value, cls_total), context)
    zero_weight = jnp.zeros((D, D), jnp.float32)
    start_totals = (zero_weight, zero_weight, zero_weight, jnp.zeros((N_NODES, OWN_DEV, D), jnp.float32))
    totals, contexts = lax.scan(per_device, start_totals, jnp.arange(N_NODES, dtype=jnp.int32))
    grad_query, grad_key, grad_value, cls_total = totals
    context = contexts.reshape(CENTRES, L, HEADS, HD).transpose(0, 2, 1, 3).reshape(CENTRES, HEADS, L * HD)
    return (context, grad_query.T, grad_key.T, grad_value.T, cls_total.reshape(OWNED, D).T)
```

```python
import functools
import math

import jax
import jax.numpy as jnp
from jax import lax
from jax.experimental import pallas as pl
from jax.experimental.pallas import tpu as pltpu
from jax.sharding import PartitionSpec as P

HD = 64
PAD = 16
LANES = 128
F32 = jnp.float32
BF16 = jnp.bfloat16
MESH = pl.DeviceIdType.MESH
VMEM_LIMIT = 56 * 1024 * 1024
ROWS_ROWS = (((1,), (1,)), ((), ()))
COLS_COLS = (((0,), (0,)), ((), ()))


def iota(shape, dim):
    return lax.broadcasted_iota(jnp.int32, shape, dim)


def ones_where(condition):
    return jnp.where(condition, 1.0, 0.0).astype(BF16)


def send(src, dst, sems, slot, axis, peer):
    return pltpu.make_async_remote_copy(
        src_ref=src,
        dst_ref=dst,
        send_sem=sems.at[0, slot],
        recv_sem=sems.at[1, slot],
        device_id={axis: peer},
        device_id_type=MESH,
    )


def greet(n, m, me, my):
    barrier = pltpu.get_barrier_semaphore()

    def hail(axis, size, here):
        def one(step, carry):
            pl.semaphore_signal(
                barrier, inc=1, device_id={axis: lax.rem(here + step, size)}, device_id_type=MESH
            )
            return carry

        lax.fori_loop(1, size, one, 0)

    hail("nodes", n, me)
    hail("mp", m, my)
    pl.semaphore_wait(barrier, n + m - 2)


def each(size, action):
    def one(step, carry):
        action(step)
        return carry

    lax.fori_loop(1, size, one, 0)


def fetch_kernel(
    n, m, cls_ref, send_ref, slot_ref, count_ref, virt_ref, mix_ref,
    slots, parts, arrived, cols, slot_sems, part_sems, col_sems,
):
    me, my = lax.axis_index("nodes"), lax.axis_index("mp")
    rows = cls_ref.shape[1]
    slot_width, pairs = slot_ref.shape
    cap = send_ref.shape[2] // 2
    greet(n, m, me, my)

    def slot_copy(step):
        return send(slot_ref, slots.at[me], slot_sems, step, "nodes", lax.rem(me + step, n))

    each(n, lambda step: slot_copy(step).start())
    slots[pl.ds(me, 1)] = slot_ref[...][None]
    each(n, lambda step: slot_copy(step).wait())

    chunk = 256
    lane = iota((cap, 2 * pairs), 1)

    def group(g, carry):
        wanted = jnp.concatenate([slots[2 * g], slots[2 * g + 1]], axis=1)
        target = iota((cap, 2 * pairs), 0) + me * cap
        total = jnp.zeros((cap, 2 * pairs), F32)
        for k in range(slot_width):
            total = total + jnp.where(target == wanted[k : k + 1, :], 1.0, 0.0)
        mixed = jnp.concatenate(
            [jnp.where(lane < pairs, total, 0.0), jnp.where(lane >= pairs, total, 0.0)], axis=0
        ).astype(BF16)
        chosen = send_ref[g]
        for r in range(0, rows, chunk):
            hot = ones_where(iota((chunk, 2 * cap), 0) + r == chosen)
            mix_ref[g, r : r + chunk, :] = jnp.dot(
                hot, mixed, preferred_element_type=F32
            ).astype(BF16)
        part = jnp.dot(cls_ref[...], mix_ref[g], preferred_element_type=F32)
        turned = part.T
        parts[2 * g] = turned[:pairs]
        parts[2 * g + 1] = turned[pairs:]
        return carry

    lax.fori_loop(0, n // 2, group, 0)

    def part_copy(step):
        peer = lax.rem(me + step, n)
        return send(parts.at[peer], arrived.at[me], part_sems, step, "nodes", peer)

    each(n, lambda step: part_copy(step).start())
    arrived[pl.ds(me, 1)] = parts[pl.ds(me, 1)]
    each(n, lambda step: part_copy(step).wait())
    total = arrived[0]
    for b in range(1, n):
        total = total + arrived[b]
    cols[pl.ds(my, 1)] = (total / count_ref[...]).astype(BF16)[None]

    def col_copy(step):
        return send(
            cols.at[my], cols.at[my], col_sems, step, "mp", lax.rem(my + step, m)
        )

    each(m, lambda step: col_copy(step).start())
    each(m, lambda step: col_copy(step).wait())
    virt_ref[...] = cols[...]


def fetch(n, m, owned_cls, send_rows, slots_t, counts):
    width, rows = owned_cls.shape
    cap = send_rows.shape[1]
    slot_width, pairs = slots_t.shape
    vmem = pl.BlockSpec(memory_space=pltpu.VMEM)
    return pl.pallas_call(
        functools.partial(fetch_kernel, n, m),
        out_shape=(
            jax.ShapeDtypeStruct((m, pairs, width), BF16),
            jax.ShapeDtypeStruct((n // 2, rows, 2 * pairs), BF16),
        ),
        in_specs=[vmem] * 4,
        out_specs=(vmem, vmem),
        scratch_shapes=[
            pltpu.VMEM((n, slot_width, pairs), jnp.int32),
            pltpu.VMEM((n, pairs, width), F32),
            pltpu.VMEM((n, pairs, width), F32),
            pltpu.VMEM((m, pairs, width), BF16),
            pltpu.SemaphoreType.DMA((2, n)),
            pltpu.SemaphoreType.DMA((2, n)),
            pltpu.SemaphoreType.DMA((2, m)),
        ],
        compiler_params=pltpu.CompilerParams(
            collective_id=1, has_side_effects=True, vmem_limit_bytes=VMEM_LIMIT
        ),
        name="fetch",
    )(owned_cls, send_rows.reshape(n // 2, 1, 2 * cap), slots_t, counts)


def attend_kernel(
    types, virt_ref, tok_ref, wq_ref, wk_ref, wv_ref, g_ref, ctx_ref, wsum_ref, vg_ref,
    tok, vpad, qs, ks, vs, kv, vv, dq, dk, dv, dkv, dvv,
):
    m, pairs, share = virt_ref.shape
    heads, centres, half, _ = g_ref.shape
    length = 2 * half
    width = heads * HD
    model = tok_ref.shape[1]
    span = length + PAD
    wide = heads * length

    spread_row = iota((centres * PAD, pairs), 0)
    spread = ones_where(
        ((spread_row // PAD) * types + spread_row % PAD == iota((centres * PAD, pairs), 1))
        & (spread_row % PAD < types)
    )
    virt = jnp.concatenate([virt_ref[i].astype(F32) for i in range(m)], axis=1).astype(BF16)
    vpad[...] = jnp.dot(spread, virt, preferred_element_type=F32).astype(BF16)
    kv[...] = lax.dot_general(
        vpad[...], wk_ref[...], ROWS_ROWS, preferred_element_type=F32
    ).astype(BF16)
    vv[...] = lax.dot_general(
        vpad[...], wv_ref[...], ROWS_ROWS, preferred_element_type=F32
    ).astype(BF16)

    block = 4 * length
    to_row, from_row = iota((block, block), 0), iota((block, block), 1)
    inside = to_row % length
    swap = ones_where(
        from_row == (to_row - inside) + jnp.where(inside < half, 2 * inside, 2 * (inside - half) + 1)
    )

    def project(i, carry):
        here = pl.ds(pl.multiple_of(i * block, block), block)
        rows = jnp.dot(swap, tok_ref[here, :], preferred_element_type=F32).astype(BF16)
        tok[here, :] = rows
        for w_ref, out in ((wq_ref, qs), (wk_ref, ks), (wv_ref, vs)):
            out[here, :] = lax.dot_general(
                rows, w_ref[...], ROWS_ROWS, preferred_element_type=F32
            ).astype(BF16)
        return carry

    lax.fori_loop(0, centres * length // block, project, 0)

    scale = 1.0 / math.sqrt(HD)
    lane_head = iota((1, width), 1) // HD
    head_lanes = [ones_where(lane_head == h) for h in range(heads)]
    own = jnp.where(
        iota((wide, width), 0) // length == iota((wide, width), 1) // HD, 1.0, 0.0
    )
    pair_lane = iota((1, 2 * HD), 1)
    left, right = ones_where(pair_lane < HD), ones_where(pair_lane >= HD)
    copies = ones_where(iota((2 * HD, width), 0) % HD == iota((2 * HD, width), 1) % HD)
    live = iota((span, wide), 0) < length + types

    def one(c):
        text = pl.ds(pl.multiple_of(c * length, length), length)
        extra = pl.ds(pl.multiple_of(c * PAD, PAD), PAD)
        q = qs[text, :]
        q_diag = jnp.concatenate([q * lanes for lanes in head_lanes], axis=0)
        k = jnp.concatenate([ks[text, :], kv[extra, :]], axis=0)
        v = jnp.concatenate([vs[text, :], vv[extra, :]], axis=0)
        g_rows = []
        for h in range(heads):
            block_g = g_ref[h, c]
            g_rows += [block_g * left, block_g * right]
        g_diag = (
            jnp.dot(jnp.concatenate(g_rows, axis=0), copies, preferred_element_type=F32) * own
        ).astype(BF16)
        scores = lax.dot_general(k, q_diag, ROWS_ROWS, preferred_element_type=F32) * scale
        scores = jnp.where(live, scores, -jnp.inf)
        grown = jnp.exp(scores - jnp.max(scores, axis=0, keepdims=True))
        probs = grown / jnp.sum(grown, axis=0, keepdims=True)
        low = probs.astype(BF16)
        prob_grads = lax.dot_general(v, g_diag, ROWS_ROWS, preferred_element_type=F32)
        dots = jnp.sum(prob_grads * probs, axis=0, keepdims=True)
        score_low = (probs * (prob_grads - dots) * scale).astype(BF16)
        dv_all = jnp.dot(low, g_diag, preferred_element_type=F32).astype(BF16)
        dk_all = jnp.dot(score_low, q_diag, preferred_element_type=F32).astype(BF16)
        dv[text, :], dvv[extra, :] = dv_all[:length], dv_all[length:]
        dk[text, :], dkv[extra, :] = dk_all[:length], dk_all[length:]
        out = (lax.dot_general(low, v, COLS_COLS, preferred_element_type=F32) * own).astype(BF16)
        flat = lax.dot_general(out, copies, ROWS_ROWS, preferred_element_type=F32)
        for h in range(heads):
            at = h * length
            ctx_ref[h, c] = jnp.where(
                pair_lane < HD, flat[at : at + half], flat[at + half : at + length]
            ).astype(BF16)
        dq_all = lax.dot_general(score_low, k, COLS_COLS, preferred_element_type=F32) * own
        dq_sum = dq_all[:length]
        for h in range(1, heads):
            dq_sum = dq_sum + dq_all[h * length : (h + 1) * length]
        dq[text, :] = dq_sum.astype(BF16)

    def several(i, carry):
        for j in range(UNROLL):
            one(i * UNROLL + j)
        return carry

    lax.fori_loop(0, centres // UNROLL, several, 0)

    part_q = lax.dot_general(dq[...], tok[...], COLS_COLS, preferred_element_type=F32)
    part_k = lax.dot_general(
        dk[...], tok[...], COLS_COLS, preferred_element_type=F32
    ) + lax.dot_general(dkv[...], vpad[...], COLS_COLS, preferred_element_type=F32)
    part_v = lax.dot_general(
        dv[...], tok[...], COLS_COLS, preferred_element_type=F32
    ) + lax.dot_general(dvv[...], vpad[...], COLS_COLS, preferred_element_type=F32)
    at = 0
    for part in (part_q, part_k, part_v):
        for lanes in range(0, model, LANES):
            wsum_ref[at : at + width, :] = part[:, lanes : lanes + LANES].astype(BF16)
            at += width
    if at < wsum_ref.shape[0]:
        wsum_ref[at:, :] = jnp.zeros((wsum_ref.shape[0] - at, LANES), BF16)
    few_k = lax.dot_general(spread, dkv[...], COLS_COLS, preferred_element_type=F32).astype(BF16)
    few_v = lax.dot_general(spread, dvv[...], COLS_COLS, preferred_element_type=F32).astype(BF16)
    vg = jnp.dot(few_k, wk_ref[...], preferred_element_type=F32) + jnp.dot(
        few_v, wv_ref[...], preferred_element_type=F32
    )
    for i in range(m):
        vg_ref[i] = vg[:, i * share : (i + 1) * share]


UNROLL = 2


def attend(total_rows, types, virt, tokens, w_query, w_key, w_value, grads):
    m, pairs, share = virt.shape
    heads, centres, half, _ = grads.shape
    count, model = tokens.shape
    width = heads * HD
    vmem = pl.BlockSpec(memory_space=pltpu.VMEM)
    extra = centres * PAD
    narrow, small = pltpu.VMEM((count, width), BF16), pltpu.VMEM((extra, width), BF16)
    return pl.pallas_call(
        functools.partial(attend_kernel, types),
        out_shape=(
            jax.ShapeDtypeStruct(grads.shape, BF16),
            jax.ShapeDtypeStruct((total_rows, LANES), BF16),
            jax.ShapeDtypeStruct((m, pairs, share), F32),
        ),
        in_specs=[vmem] * 6,
        out_specs=(vmem, vmem, vmem),
        scratch_shapes=[
            pltpu.VMEM((count, model), BF16), pltpu.VMEM((extra, model), BF16),
            narrow, narrow, narrow, small, small, narrow, narrow, narrow, small, small,
        ],
        compiler_params=pltpu.CompilerParams(vmem_limit_bytes=VMEM_LIMIT),
        name="attend",
    )(virt, tokens, w_query, w_key, w_value, grads)


def reduce_kernel(
    n, m, wsum_ref, vg_ref, count_ref, weights_ref, shared_ref,
    w_in, w_all, vg_in, shared, vg_sems, sh_sems, rs_sems, ag_sems,
):
    me, my = lax.axis_index("nodes"), lax.axis_index("mp")
    chunk = w_in.shape[1]
    greet(n, m, me, my)

    def vg_copy(step):
        peer = lax.rem(my + step, m)
        return send(vg_ref.at[peer], vg_in.at[my], vg_sems, step, "mp", peer)

    def rs_copy(step):
        peer = lax.rem(me + step, n)
        return send(wsum_ref.at[peer], w_in.at[me], rs_sems, step, "nodes", peer)

    def sh_copy(step):
        return send(shared.at[me], shared.at[me], sh_sems, step, "nodes", lax.rem(me + step, n))

    def ag_copy(step):
        return send(w_all.at[me], w_all.at[me], ag_sems, step, "nodes", lax.rem(me + step, n))

    each(m, lambda step: vg_copy(step).start())
    each(n, lambda step: rs_copy(step).start())
    vg_in[pl.ds(my, 1)] = vg_ref[pl.ds(my, 1)]
    w_in[pl.ds(me, 1)] = wsum_ref[pl.ds(me, 1)]
    each(m, lambda step: vg_copy(step).wait())
    total = vg_in[0]
    for i in range(1, m):
        total = total + vg_in[i]
    shared[pl.ds(me, 1)] = (total / count_ref[...]).astype(BF16)[None]
    each(n, lambda step: sh_copy(step).start())
    each(n, lambda step: rs_copy(step).wait())
    weights = w_in[0].astype(F32)
    for b in range(1, n):
        weights = weights + w_in[b].astype(F32)
    w_all[pl.ds(me, 1)] = weights.astype(BF16)[None]
    each(n, lambda step: ag_copy(step).start())
    each(n, lambda step: sh_copy(step).wait())
    shared_ref[...] = shared[...]
    each(n, lambda step: ag_copy(step).wait())
    weights_ref[...] = w_all[...]


def reduce_all(n, m, wsum, vg, counts):
    chunk = wsum.shape[0] // n
    _, pairs, share = vg.shape
    vmem = pl.BlockSpec(memory_space=pltpu.VMEM)
    return pl.pallas_call(
        functools.partial(reduce_kernel, n, m),
        out_shape=(
            jax.ShapeDtypeStruct((n, chunk, LANES), BF16),
            jax.ShapeDtypeStruct((n, pairs, share), BF16),
        ),
        in_specs=[vmem] * 3,
        out_specs=(vmem, vmem),
        scratch_shapes=[
            pltpu.VMEM((n, chunk, LANES), BF16),
            pltpu.VMEM((n, chunk, LANES), BF16),
            pltpu.VMEM((m, pairs, share), F32),
            pltpu.VMEM((n, pairs, share), BF16),
            pltpu.SemaphoreType.DMA((2, m)),
            pltpu.SemaphoreType.DMA((2, n)),
            pltpu.SemaphoreType.DMA((2, n)),
            pltpu.SemaphoreType.DMA((2, n)),
        ],
        compiler_params=pltpu.CompilerParams(
            collective_id=2, has_side_effects=True, vmem_limit_bytes=VMEM_LIMIT
        ),
        name="reduce",
    )(wsum.reshape(n, chunk, LANES), vg, counts)


def finish_kernel(weights_ref, shared_ref, mix_ref, q_ref, k_ref, v_ref, cls_ref):
    width, model = q_ref.shape
    groups = mix_ref.shape[0]
    at = 0
    for out in (q_ref, k_ref, v_ref):
        for lanes in range(0, model, LANES):
            out[:, lanes : lanes + LANES] = weights_ref[at : at + width, :].astype(F32)
            at += width

    def group(g, carry):
        both = jnp.concatenate([shared_ref[2 * g], shared_ref[2 * g + 1]], axis=0)
        turned = both.astype(F32).T.astype(BF16)
        part = lax.dot_general(turned, mix_ref[g], ROWS_ROWS, preferred_element_type=F32)

        @pl.when(g == 0)
        def _():
            cls_ref[...] = part

        @pl.when(g > 0)
        def _():
            cls_ref[...] += part

        return carry

    lax.fori_loop(0, groups, group, 0)


def finish(weights, shared, mix, width, model):
    vmem = pl.BlockSpec(memory_space=pltpu.VMEM)
    weight = jax.ShapeDtypeStruct((width, model), F32)
    rows = mix.shape[1]
    return pl.pallas_call(
        finish_kernel,
        out_shape=(weight, weight, weight, jax.ShapeDtypeStruct((shared.shape[2], rows), F32)),
        in_specs=[vmem] * 3,
        out_specs=(vmem,) * 4,
        compiler_params=pltpu.CompilerParams(vmem_limit_bytes=VMEM_LIMIT),
        name="finish",
    )(weights, shared, mix)


def body(n, m, tokens, w_query, w_key, w_value, grad_out, owned_cls, send_rows, neigh_slot, neigh_count):
    centres, length, model = tokens.shape
    width = w_query.shape[0]
    heads = width // HD
    types, slot_width = neigh_slot.shape[1:]
    pairs = centres * types
    live = lax.broadcasted_iota(jnp.int32, neigh_slot.shape, 2) < neigh_count[:, :, None]
    slots_t = jnp.where(live, neigh_slot, -1).reshape(pairs, slot_width).T
    counts = neigh_count.reshape(pairs, 1).astype(F32)
    virt, mix = fetch(n, m, owned_cls, send_rows[0], slots_t, counts)
    grads = grad_out.transpose(1, 0, 2).reshape(heads, centres, length // 2, 2 * HD)
    pieces = 3 * width * (model // LANES)
    chunk = -(-pieces // (n * 16)) * 16
    context, wsum, vg = attend(
        n * chunk, types, virt, tokens.reshape(-1, model), w_query, w_key, w_value, grads
    )
    weights, shared = reduce_all(n, m, wsum, vg, counts)
    grad_q, grad_k, grad_v, grad_cls = finish(
        weights.reshape(n * chunk, LANES), shared, mix, width, model
    )
    context = context.reshape(heads, centres, length * HD).transpose(1, 0, 2)
    return context, grad_q, grad_k, grad_v, grad_cls


def solution(mesh):
    in_specs = (
        P("nodes", None, None),
        P("mp", None),
        P("mp", None),
        P("mp", None),
        P("nodes", "mp", None),
        P("mp", "nodes"),
        P("nodes", None, None),
        P("nodes", None, None),
        P("nodes", None),
    )
    out_specs = (
        P("nodes", "mp", None),
        P("mp", None),
        P("mp", None),
        P("mp", None),
        P("mp", "nodes"),
    )
    return jax.shard_map(
        functools.partial(body, mesh.shape["nodes"], mesh.shape["mp"]),
        mesh=mesh, in_specs=in_specs, out_specs=out_specs, check_vma=False,
    )
```

```python
import functools
import math

import jax
import jax.numpy as jnp
from jax import lax
from jax.experimental import pallas as pl
from jax.experimental.pallas import tpu as pltpu
from jax.sharding import PartitionSpec as P

HD = 64
PAD = 16
LANES = 128
F32 = jnp.float32
BF16 = jnp.bfloat16
MESH = pl.DeviceIdType.MESH
VMEM_LIMIT = 56 * 1024 * 1024
ROWS_ROWS = (((1,), (1,)), ((), ()))
COLS_COLS = (((0,), (0,)), ((), ()))


def iota(shape, dim):
    return lax.broadcasted_iota(jnp.int32, shape, dim)


def ones_where(condition):
    return jnp.where(condition, 1.0, 0.0).astype(BF16)


def send(src, dst, sems, slot, axis, peer):
    return pltpu.make_async_remote_copy(
        src_ref=src,
        dst_ref=dst,
        send_sem=sems.at[(0, *slot)],
        recv_sem=sems.at[(1, *slot)],
        device_id={axis: peer},
        device_id_type=MESH,
    )


def greet(n, m, me, my):
    barrier = pltpu.get_barrier_semaphore()

    def hail(axis, size, here):
        def one(step, carry):
            pl.semaphore_signal(
                barrier, inc=1, device_id={axis: lax.rem(here + step, size)}, device_id_type=MESH
            )
            return carry

        lax.fori_loop(1, size, one, 0)

    hail("nodes", n, me)
    hail("mp", m, my)
    pl.semaphore_wait(barrier, n + m - 2)


def each(size, action):
    def one(step, carry):
        action(step)
        return carry

    lax.fori_loop(1, size, one, 0)


UNROLL = 2


def layer_kernel(
    n, m, types,
    tok_ref, wq_ref, wk_ref, wv_ref, g_ref, cls_ref, send_ref, slot_ref, count_ref,
    ctx_ref, weights_ref, shared_ref, mix_ref,
    slots_own, slots, parts, arrived, cols,
    tok, vpad, qs, ks, vs, kv, vv, dq, dk, dv, dkv, dvv, lows,
    wsum, x_in, z_sum, z_in, w_all, vg_out, vg_in, shared,
    slot_sems, part_sems, col_sems, vg_sems, sh_sems, x_sems, z_sems, a_sems, f_sems,
):
    me, my = lax.axis_index("nodes"), lax.axis_index("mp")
    zs = n // 2
    par, zz = lax.rem(me, 2), lax.div(me, 2)
    mate = me + 1 - 2 * par
    rows = cls_ref.shape[1]
    cap = send_ref.shape[1]
    centres, _, slot_width = slot_ref.shape
    pairs = centres * types
    heads, _, half, _ = g_ref.shape
    length = 2 * half
    width = heads * HD
    model = tok_ref.shape[1]
    share = model // m
    span = length + PAD
    wide = heads * length

    counts = count_ref[...].astype(F32)
    lists = []
    for t in range(types):
        turned = slot_ref[:, t, :].astype(F32).T
        spot = iota((slot_width, centres), 0).astype(F32)
        lists.append(jnp.where(spot < counts[t : t + 1, :], turned, -1.0))
    slots_own[...] = jnp.concatenate(lists, axis=1)
    count_row = jnp.concatenate([counts[t : t + 1, :] for t in range(types)], axis=1)
    count_col = jnp.broadcast_to(count_row, (8, pairs)).T[:, :1]

    greet(n, m, me, my)

    def slot_copy(step):
        return send(slots_own, slots.at[me], slot_sems, (step,), "nodes", lax.rem(me + step, n))

    each(n, lambda step: slot_copy(step).start())
    slots[pl.ds(me, 1)] = slots_own[...][None]

    block = 4 * length
    to_row, from_row = iota((block, block), 0), iota((block, block), 1)
    inside = to_row % length
    swap = ones_where(
        from_row == (to_row - inside) + jnp.where(inside < half, 2 * inside, 2 * (inside - half) + 1)
    )

    def project(i, carry):
        here = pl.ds(pl.multiple_of(i * block, block), block)
        moved = jnp.dot(swap, tok_ref[here, :], preferred_element_type=F32).astype(BF16)
        tok[here, :] = moved
        for w_ref, out in ((wq_ref, qs), (wk_ref, ks), (wv_ref, vs)):
            out[here, :] = lax.dot_general(
                moved, w_ref[...], ROWS_ROWS, preferred_element_type=F32
            ).astype(BF16)
        return carry

    blocks = centres * length // block
    lax.fori_loop(0, blocks // 2, project, 0)
    each(n, lambda step: slot_copy(step).wait())

    chunk = 256
    lane = iota((cap, 2 * pairs), 1)
    target = (iota((cap, 2 * pairs), 0) + me * cap).astype(F32)

    def group(g, carry):
        wanted = jnp.concatenate([slots[2 * g], slots[2 * g + 1]], axis=1)
        total = jnp.zeros((cap, 2 * pairs), F32)
        for k in range(slot_width):
            total = total + jnp.where(target == wanted[k : k + 1, :], 1.0, 0.0)
        mixed = jnp.concatenate(
            [jnp.where(lane < pairs, total, 0.0), jnp.where(lane >= pairs, total, 0.0)], axis=0
        ).astype(BF16)
        chosen = jnp.concatenate(
            [send_ref[pl.ds(2 * g, 1), :], send_ref[pl.ds(2 * g + 1, 1), :]], axis=1
        )
        for r in range(0, rows, chunk):
            hot = ones_where(iota((chunk, 2 * cap), 0) + r == chosen)
            mix_ref[g, r : r + chunk, :] = jnp.dot(
                hot, mixed, preferred_element_type=F32
            ).astype(BF16)
        turned = jnp.dot(cls_ref[...], mix_ref[g], preferred_element_type=F32).T
        parts[2 * g] = turned[:pairs]
        parts[2 * g + 1] = turned[pairs:]
        return carry

    lax.fori_loop(0, n // 2, group, 0)

    def part_copy(step):
        peer = lax.rem(me + step, n)
        return send(parts.at[peer], arrived.at[me], part_sems, (step,), "nodes", peer)

    each(n, lambda step: part_copy(step).start())
    arrived[pl.ds(me, 1)] = parts[pl.ds(me, 1)]
    lax.fori_loop(blocks // 2, blocks, project, 0)
    each(n, lambda step: part_copy(step).wait())
    total = arrived[0]
    for b in range(1, n):
        total = total + arrived[b]
    cols[pl.ds(my, 1)] = (total / count_col).astype(BF16)[None]

    def col_copy(step):
        return send(cols.at[my], cols.at[my], col_sems, (step,), "mp", lax.rem(my + step, m))

    each(m, lambda step: col_copy(step).start())
    spread_row = iota((centres * PAD, pairs), 0)
    spread = ones_where(
        ((spread_row % PAD) * centres + spread_row // PAD == iota((centres * PAD, pairs), 1))
        & (spread_row % PAD < types)
    )
    each(m, lambda step: col_copy(step).wait())
    virt = jnp.concatenate([cols[i].astype(F32) for i in range(m)], axis=1).astype(BF16)
    vpad[...] = jnp.dot(spread, virt, preferred_element_type=F32).astype(BF16)
    kv[...] = lax.dot_general(
        vpad[...], wk_ref[...], ROWS_ROWS, preferred_element_type=F32
    ).astype(BF16)
    vv[...] = lax.dot_general(
        vpad[...], wv_ref[...], ROWS_ROWS, preferred_element_type=F32
    ).astype(BF16)

    def x_copy(p):
        return send(wsum.at[p, 1 - par], x_in.at[p], x_sems, (p,), "nodes", mate)

    def z_copy(p, step):
        peer = lax.rem(zz + step, zs)
        return send(z_sum.at[p, peer], z_in.at[p, zz], z_sems, (p, step), "nodes", 2 * peer + par)

    def a_copy(p, step):
        own = w_all.at[p, par, zz]
        return send(own, own, a_sems, (p, step), "nodes", 2 * lax.rem(zz + step, zs) + par)

    def f_copy(p, step):
        held = w_all.at[p, par, lax.rem(zz - step + zs, zs)]
        return send(held, held, f_sems, (p, step), "nodes", mate)

    def part_ready(p, part):
        at = 0
        flat = []
        for lanes in range(0, model, LANES):
            flat.append(part[:, lanes : lanes + LANES].astype(BF16))
        flat = jnp.concatenate(flat, axis=0)
        _, _, _, size, _ = wsum.shape
        short = 2 * zs * size - flat.shape[0]
        if short:
            flat = jnp.concatenate([flat, jnp.zeros((short, LANES), BF16)], axis=0)
        wsum[p] = flat.reshape(2, zs, size, LANES)
        x_copy(p).start()

    def x_done(p):
        x_copy(p).wait()
        z_sum[p] = (wsum[p, par].astype(F32) + x_in[p].astype(F32)).astype(BF16)
        each(zs, lambda step: z_copy(p, step).start())
        z_in[p, pl.ds(zz, 1)] = z_sum[p, pl.ds(zz, 1)]

    def z_done(p):
        each(zs, lambda step: z_copy(p, step).wait())
        weights = z_in[p, 0].astype(F32)
        for b in range(1, zs):
            weights = weights + z_in[p, b].astype(F32)
        w_all[p, par, zz] = weights.astype(BF16)
        each(zs, lambda step: a_copy(p, step).start())
        f_copy(p, 0).start()

    def a_done(p):
        def forward(step):
            a_copy(p, step).wait()
            f_copy(p, step).start()

        each(zs, forward)

    def f_done(p):
        f_copy(p, 0).wait()
        each(zs, lambda step: f_copy(p, step).wait())

    scale = 1.0 / math.sqrt(HD)
    lane_head = iota((1, width), 1) // HD
    head_lanes = [ones_where(lane_head == h) for h in range(heads)]
    own = jnp.where(
        iota((wide, width), 0) // length == iota((wide, width), 1) // HD, 1.0, 0.0
    )
    pair_lane = iota((1, 2 * HD), 1)
    left, right = ones_where(pair_lane < HD), ones_where(pair_lane >= HD)
    copies = ones_where(iota((2 * HD, width), 0) % HD == iota((2 * HD, width), 1) % HD)
    live = iota((span, wide), 0) < length + types

    def places(c):
        return (
            pl.ds(pl.multiple_of(c * length, length), length),
            pl.ds(pl.multiple_of(c * PAD, PAD), PAD),
            pl.ds(pl.multiple_of(c * span, PAD), span),
        )

    def diagonal(text):
        q = qs[text, :]
        return jnp.concatenate([q * lanes for lanes in head_lanes], axis=0)

    def forward_values(c):
        text, extra, both = places(c)
        q_diag = diagonal(text)
        k = jnp.concatenate([ks[text, :], kv[extra, :]], axis=0)
        v = jnp.concatenate([vs[text, :], vv[extra, :]], axis=0)
        g_rows = []
        for h in range(heads):
            block_g = g_ref[h, c]
            g_rows += [block_g * left, block_g * right]
        g_diag = (
            jnp.dot(jnp.concatenate(g_rows, axis=0), copies, preferred_element_type=F32) * own
        ).astype(BF16)
        scores = lax.dot_general(k, q_diag, ROWS_ROWS, preferred_element_type=F32) * scale
        scores = jnp.where(live, scores, -jnp.inf)
        grown = jnp.exp(scores - jnp.max(scores, axis=0, keepdims=True))
        probs = grown / jnp.sum(grown, axis=0, keepdims=True)
        low = probs.astype(BF16)
        prob_grads = lax.dot_general(v, g_diag, ROWS_ROWS, preferred_element_type=F32)
        dots = jnp.sum(prob_grads * probs, axis=0, keepdims=True)
        lows[both, :] = (probs * (prob_grads - dots) * scale).astype(BF16)
        dv_all = jnp.dot(low, g_diag, preferred_element_type=F32).astype(BF16)
        dv[text, :], dvv[extra, :] = dv_all[:length], dv_all[length:]
        out = (lax.dot_general(low, v, COLS_COLS, preferred_element_type=F32) * own).astype(BF16)
        flat = lax.dot_general(out, copies, ROWS_ROWS, preferred_element_type=F32)
        for h in range(heads):
            at = h * length
            ctx_ref[h, c] = jnp.where(
                pair_lane < HD, flat[at : at + half], flat[at + half : at + length]
            ).astype(BF16)

    def key_side(c):
        text, extra, both = places(c)
        dk_all = jnp.dot(lows[both, :], diagonal(text), preferred_element_type=F32).astype(BF16)
        dk[text, :], dkv[extra, :] = dk_all[:length], dk_all[length:]

    def query_side(c):
        text, extra, both = places(c)
        k = jnp.concatenate([ks[text, :], kv[extra, :]], axis=0)
        dq_all = lax.dot_general(lows[both, :], k, COLS_COLS, preferred_element_type=F32) * own
        dq_sum = dq_all[:length]
        for h in range(1, heads):
            dq_sum = dq_sum + dq_all[h * length : (h + 1) * length]
        dq[text, :] = dq_sum.astype(BF16)

    def over_centres(action, unroll):
        def several(i, carry):
            for j in range(unroll):
                action(i * unroll + j)
            return carry

        lax.fori_loop(0, centres // unroll, several, 0)

    def weight_part(grads, extra):
        part = lax.dot_general(grads[...], tok[...], COLS_COLS, preferred_element_type=F32)
        if extra is not None:
            part += lax.dot_general(extra[...], vpad[...], COLS_COLS, preferred_element_type=F32)
        return part

    over_centres(forward_values, UNROLL)
    part_ready(2, weight_part(dv, dvv))
    over_centres(key_side, 2 * UNROLL)
    part_ready(1, weight_part(dk, dkv))
    few_k = lax.dot_general(spread, dkv[...], COLS_COLS, preferred_element_type=F32).astype(BF16)
    few_v = lax.dot_general(spread, dvv[...], COLS_COLS, preferred_element_type=F32).astype(BF16)
    vg = jnp.dot(few_k, wk_ref[...], preferred_element_type=F32) + jnp.dot(
        few_v, wv_ref[...], preferred_element_type=F32
    )
    for i in range(m):
        vg_out[i] = vg[:, i * share : (i + 1) * share]

    def vg_copy(step):
        peer = lax.rem(my + step, m)
        return send(vg_out.at[peer], vg_in.at[my], vg_sems, (step,), "mp", peer)

    def sh_copy(step):
        held = shared.at[me]
        return send(held, held, sh_sems, (step,), "nodes", lax.rem(me + step, n))

    each(m, lambda step: vg_copy(step).start())
    vg_in[pl.ds(my, 1)] = vg_out[pl.ds(my, 1)]
    x_done(2)
    over_centres(query_side, 2 * UNROLL)
    part_ready(0, weight_part(dq, None))
    each(m, lambda step: vg_copy(step).wait())
    total = vg_in[0]
    for i in range(1, m):
        total = total + vg_in[i]
    shared[pl.ds(me, 1)] = (total / count_col).astype(BF16)[None]
    each(n, lambda step: sh_copy(step).start())
    x_done(1)
    z_done(2)
    x_done(0)
    z_done(1)
    a_done(2)
    z_done(0)
    a_done(1)
    each(n, lambda step: sh_copy(step).wait())
    shared_ref[...] = shared[...]
    a_done(0)
    for p in (2, 1, 0):
        f_done(p)
    weights_ref[...] = w_all[...]


def layer(n, m, types, tokens, w_query, w_key, w_value, grads, owned_cls, send_rows, slots, counts):
    heads, centres, half, _ = grads.shape
    count, model = tokens.shape
    width = heads * HD
    pairs, slot_width, rows = centres * types, slots.shape[2], owned_cls.shape[1]
    share = owned_cls.shape[0]
    vmem = pl.BlockSpec(memory_space=pltpu.VMEM)
    extra = centres * PAD
    zs = n // 2
    chunk = -(-(width * (model // LANES)) // (n * 16)) * 16
    narrow, small = pltpu.VMEM((count, width), BF16), pltpu.VMEM((extra, width), BF16)
    near = pltpu.VMEM((3, zs, chunk, LANES), BF16)
    all_parts = (3, 2, zs, chunk, LANES)
    dma = pltpu.SemaphoreType.DMA
    return pl.pallas_call(
        functools.partial(layer_kernel, n, m, types),
        out_shape=(
            jax.ShapeDtypeStruct(grads.shape, BF16),
            jax.ShapeDtypeStruct(all_parts, BF16),
            jax.ShapeDtypeStruct((n, pairs, share), BF16),
            jax.ShapeDtypeStruct((zs, rows, 2 * pairs), BF16),
        ),
        in_specs=[vmem] * 9,
        out_specs=(vmem,) * 4,
        scratch_shapes=[
            pltpu.VMEM((slot_width, pairs), F32),
            pltpu.VMEM((n, slot_width, pairs), F32),
            pltpu.VMEM((n, pairs, share), F32),
            pltpu.VMEM((n, pairs, share), F32),
            pltpu.VMEM((m, pairs, share), BF16),
            pltpu.VMEM((count, model), BF16), pltpu.VMEM((extra, model), BF16),
            narrow, narrow, narrow, small, small, narrow, narrow, narrow, small, small,
            pltpu.VMEM((count + extra, width), BF16),
            pltpu.VMEM(all_parts, BF16), near, near, near, pltpu.VMEM(all_parts, BF16),
            pltpu.VMEM((m, pairs, share), F32), pltpu.VMEM((m, pairs, share), F32),
            pltpu.VMEM((n, pairs, share), BF16),
            dma((2, n)), dma((2, n)), dma((2, m)), dma((2, m)), dma((2, n)),
            dma((2, 3)), dma((2, 3, zs)), dma((2, 3, zs)), dma((2, 3, zs)),
        ],
        compiler_params=pltpu.CompilerParams(
            collective_id=1, has_side_effects=True, vmem_limit_bytes=VMEM_LIMIT
        ),
        name="layer",
    )(tokens, w_query, w_key, w_value, grads, owned_cls, send_rows, slots, counts)


STEPS = 2


def finish_kernel(weights_ref, shared_ref, mix_ref, q_ref, k_ref, v_ref, cls_ref):
    width, model = q_ref.shape
    groups = mix_ref.shape[0]
    for p, out in enumerate((q_ref, k_ref, v_ref)):
        for i in range(model // LANES):
            out[:, i * LANES : (i + 1) * LANES] = weights_ref[
                p, i * width : (i + 1) * width, :
            ].astype(F32)

    def product(g):
        both = jnp.concatenate([shared_ref[2 * g], shared_ref[2 * g + 1]], axis=0)
        turned = both.astype(F32).T.astype(BF16)
        return lax.dot_general(turned, mix_ref[g], ROWS_ROWS, preferred_element_type=F32)

    cls_ref[...] = product(0)

    def group(g, carry):
        cls_ref[...] += product(g)
        return carry

    lax.fori_loop(1, groups, group, 0)


def finish(weights, shared, mix, width, model):
    weight = jax.ShapeDtypeStruct((width, model), F32)
    groups, rows, lanes = mix.shape
    share = shared.shape[2]
    part = width * model // LANES // STEPS
    weight_spec = pl.BlockSpec((width, model // STEPS), lambda i: (0, i))
    return pl.pallas_call(
        finish_kernel,
        grid=(STEPS,),
        out_shape=(weight, weight, weight, jax.ShapeDtypeStruct((share, rows), F32)),
        in_specs=[
            pl.BlockSpec((3, part, LANES), lambda i: (0, i, 0)),
            pl.BlockSpec(shared.shape, lambda i: (0, 0, 0)),
            pl.BlockSpec((groups, rows // STEPS, lanes), lambda i: (0, i, 0)),
        ],
        out_specs=(weight_spec, weight_spec, weight_spec,
                   pl.BlockSpec((share, rows // STEPS), lambda i: (0, i))),
        compiler_params=pltpu.CompilerParams(vmem_limit_bytes=VMEM_LIMIT),
        name="finish",
    )(weights, shared, mix)


def body(n, m, tokens, w_query, w_key, w_value, grad_out, owned_cls, send_rows, neigh_slot, neigh_count):
    centres, length, model = tokens.shape
    width = w_query.shape[0]
    heads = width // HD
    grads = grad_out.transpose(1, 0, 2).reshape(heads, centres, length // 2, 2 * HD)
    context, weights, shared, mix = layer(
        n, m, neigh_slot.shape[1], tokens.reshape(-1, model), w_query, w_key, w_value, grads,
        owned_cls, send_rows[0], neigh_slot, neigh_count.T,
    )
    grad_q, grad_k, grad_v, grad_cls = finish(
        weights.reshape(3, -1, LANES), shared, mix, width, model
    )
    context = context.reshape(heads, centres, length * HD).transpose(1, 0, 2)
    return context, grad_q, grad_k, grad_v, grad_cls


def solution(mesh):
    in_specs = (
        P("nodes", None, None),
        P("mp", None),
        P("mp", None),
        P("mp", None),
        P("nodes", "mp", None),
        P("mp", "nodes"),
        P("nodes", None, None),
        P("nodes", None, None),
        P("nodes", None),
    )
    out_specs = (
        P("nodes", "mp", None),
        P("mp", None),
        P("mp", None),
        P("mp", None),
        P("mp", "nodes"),
    )
    return jax.shard_map(
        functools.partial(body, mesh.shape["nodes"], mesh.shape["mp"]),
        mesh=mesh, in_specs=in_specs, out_specs=out_specs, check_vma=False,
    )
```

```python
import functools
import math

import jax
import jax.numpy as jnp
from jax import lax
from jax.experimental import pallas as pl
from jax.experimental.pallas import tpu as pltpu
from jax.sharding import PartitionSpec as P

HD = 64
PAD = 16
LANES = 128
F32 = jnp.float32
BF16 = jnp.bfloat16
MESH = pl.DeviceIdType.MESH
VMEM_LIMIT = 56 * 1024 * 1024
ROWS_ROWS = (((1,), (1,)), ((), ()))
COLS_COLS = (((0,), (0,)), ((), ()))


def iota(shape, dim):
    return lax.broadcasted_iota(jnp.int32, shape, dim)


def ones_where(condition):
    return jnp.where(condition, 1.0, 0.0).astype(BF16)


def send(src, dst, sems, slot, axis, peer):
    return pltpu.make_async_remote_copy(
        src_ref=src,
        dst_ref=dst,
        send_sem=sems.at[(0, *slot)],
        recv_sem=sems.at[(1, *slot)],
        device_id={axis: peer},
        device_id_type=MESH,
    )


def greet(n, m, me, my):
    barrier = pltpu.get_barrier_semaphore()

    def hail(axis, size, here):
        def one(step, carry):
            pl.semaphore_signal(
                barrier, inc=1, device_id={axis: lax.rem(here + step, size)}, device_id_type=MESH
            )
            return carry

        lax.fori_loop(1, size, one, 0)

    hail("nodes", n, me)
    hail("mp", m, my)
    pl.semaphore_wait(barrier, n + m - 2)


def each(size, action):
    def one(step, carry):
        action(step)
        return carry

    lax.fori_loop(1, size, one, 0)


UNROLL = 4


def layer_kernel(
    n, m, types,
    tok_ref, wq_ref, wk_ref, wv_ref, g_ref, cls_ref, send_ref, slot_ref, count_ref,
    ctx_ref, weights_ref, shared_ref, mix_ref,
    slots_own, slots, parts, arrived, cols,
    tok, vpad, qs, ks, vs, kv, vv, dq, dk, dv, dkv, dvv, lows, probs_all, g_all,
    wsum, x_in, z_sum, z_in, w_all, vg_out, vg_in, shared,
    slot_sems, part_sems, col_sems, vg_sems, sh_sems, x_sems, z_sems, a_sems, f_sems,
):
    me, my = lax.axis_index("nodes"), lax.axis_index("mp")
    zs = n // 2
    par, zz = lax.rem(me, 2), lax.div(me, 2)
    mate = me + 1 - 2 * par
    rows = cls_ref.shape[1]
    cap = send_ref.shape[1]
    centres, _, slot_width = slot_ref.shape
    pairs = centres * types
    heads, _, half, _ = g_ref.shape
    length = 2 * half
    width = heads * HD
    model = tok_ref.shape[1]
    share = model // m
    span = length + PAD
    wide = heads * length

    counts = count_ref[...].astype(F32)
    lists = []
    for t in range(types):
        turned = slot_ref[:, t, :].astype(F32).T
        spot = iota((slot_width, centres), 0).astype(F32)
        lists.append(jnp.where(spot < counts[t : t + 1, :], turned, -1.0))
    slots_own[...] = jnp.concatenate(lists, axis=1)
    count_row = jnp.concatenate([counts[t : t + 1, :] for t in range(types)], axis=1)
    count_col = jnp.broadcast_to(count_row, (8, pairs)).T[:, :1]

    greet(n, m, me, my)

    def slot_copy(step):
        return send(slots_own, slots.at[me], slot_sems, (step,), "nodes", lax.rem(me + step, n))

    each(n, lambda step: slot_copy(step).start())
    slots[pl.ds(me, 1)] = slots_own[...][None]

    block = 4 * length
    to_row, from_row = iota((block, block), 0), iota((block, block), 1)
    inside = to_row % length
    swap = ones_where(
        from_row == (to_row - inside) + jnp.where(inside < half, 2 * inside, 2 * (inside - half) + 1)
    )

    def project(i, carry):
        here = pl.ds(pl.multiple_of(i * block, block), block)
        moved = jnp.dot(swap, tok_ref[here, :], preferred_element_type=F32).astype(BF16)
        tok[here, :] = moved
        for w_ref, out in ((wq_ref, qs), (wk_ref, ks), (wv_ref, vs)):
            out[here, :] = lax.dot_general(
                moved, w_ref[...], ROWS_ROWS, preferred_element_type=F32
            ).astype(BF16)
        return carry

    blocks = centres * length // block
    lax.fori_loop(0, blocks // 2, project, 0)
    each(n, lambda step: slot_copy(step).wait())

    chunk = 256
    lane = iota((cap, 2 * pairs), 1)
    target = (iota((cap, 2 * pairs), 0) + me * cap).astype(F32)

    def group(g, carry):
        wanted = jnp.concatenate([slots[2 * g], slots[2 * g + 1]], axis=1)
        total = jnp.zeros((cap, 2 * pairs), F32)
        for k in range(slot_width):
            total = total + jnp.where(target == wanted[k : k + 1, :], 1.0, 0.0)
        mixed = jnp.concatenate(
            [jnp.where(lane < pairs, total, 0.0), jnp.where(lane >= pairs, total, 0.0)], axis=0
        ).astype(BF16)
        chosen = jnp.concatenate(
            [send_ref[pl.ds(2 * g, 1), :], send_ref[pl.ds(2 * g + 1, 1), :]], axis=1
        )
        for r in range(0, rows, chunk):
            hot = ones_where(iota((chunk, 2 * cap), 0) + r == chosen)
            mix_ref[g, r : r + chunk, :] = jnp.dot(
                hot, mixed, preferred_element_type=F32
            ).astype(BF16)
        turned = jnp.dot(cls_ref[...], mix_ref[g], preferred_element_type=F32).T
        parts[2 * g] = turned[:pairs]
        parts[2 * g + 1] = turned[pairs:]
        return carry

    lax.fori_loop(0, n // 2, group, 0)

    def part_copy(step):
        peer = lax.rem(me + step, n)
        return send(parts.at[peer], arrived.at[me], part_sems, (step,), "nodes", peer)

    each(n, lambda step: part_copy(step).start())
    arrived[pl.ds(me, 1)] = parts[pl.ds(me, 1)]
    lax.fori_loop(blocks // 2, blocks, project, 0)
    each(n, lambda step: part_copy(step).wait())
    total = arrived[0]
    for b in range(1, n):
        total = total + arrived[b]
    cols[pl.ds(my, 1)] = (total / count_col).astype(BF16)[None]

    def col_copy(step):
        return send(cols.at[my], cols.at[my], col_sems, (step,), "mp", lax.rem(my + step, m))

    each(m, lambda step: col_copy(step).start())
    spread_row = iota((centres * PAD, pairs), 0)
    spread = ones_where(
        ((spread_row % PAD) * centres + spread_row // PAD == iota((centres * PAD, pairs), 1))
        & (spread_row % PAD < types)
    )
    each(m, lambda step: col_copy(step).wait())
    virt = jnp.concatenate([cols[i].astype(F32) for i in range(m)], axis=1).astype(BF16)
    vpad[...] = jnp.dot(spread, virt, preferred_element_type=F32).astype(BF16)
    kv[...] = lax.dot_general(
        vpad[...], wk_ref[...], ROWS_ROWS, preferred_element_type=F32
    ).astype(BF16)
    vv[...] = lax.dot_general(
        vpad[...], wv_ref[...], ROWS_ROWS, preferred_element_type=F32
    ).astype(BF16)

    def x_copy(p):
        return send(wsum.at[p, 1 - par], x_in.at[p], x_sems, (p,), "nodes", mate)

    def z_copy(p, step):
        peer = lax.rem(zz + step, zs)
        return send(z_sum.at[p, peer], z_in.at[p, zz], z_sems, (p, step), "nodes", 2 * peer + par)

    def a_copy(p, step):
        own = w_all.at[p, par, zz]
        return send(own, own, a_sems, (p, step), "nodes", 2 * lax.rem(zz + step, zs) + par)

    def f_copy(p, step):
        held = w_all.at[p, par, lax.rem(zz - step + zs, zs)]
        return send(held, held, f_sems, (p, step), "nodes", mate)

    def part_ready(p, part):
        at = 0
        flat = []
        for lanes in range(0, model, LANES):
            flat.append(part[:, lanes : lanes + LANES].astype(BF16))
        flat = jnp.concatenate(flat, axis=0)
        _, _, _, size, _ = wsum.shape
        short = 2 * zs * size - flat.shape[0]
        if short:
            flat = jnp.concatenate([flat, jnp.zeros((short, LANES), BF16)], axis=0)
        wsum[p] = flat.reshape(2, zs, size, LANES)
        x_copy(p).start()

    def x_done(p):
        x_copy(p).wait()
        z_sum[p] = (wsum[p, par].astype(F32) + x_in[p].astype(F32)).astype(BF16)
        each(zs, lambda step: z_copy(p, step).start())
        z_in[p, pl.ds(zz, 1)] = z_sum[p, pl.ds(zz, 1)]

    def z_done(p):
        each(zs, lambda step: z_copy(p, step).wait())
        weights = z_in[p, 0].astype(F32)
        for b in range(1, zs):
            weights = weights + z_in[p, b].astype(F32)
        w_all[p, par, zz] = weights.astype(BF16)
        each(zs, lambda step: a_copy(p, step).start())
        f_copy(p, 0).start()

    def a_done(p):
        def forward(step):
            a_copy(p, step).wait()
            f_copy(p, step).start()

        each(zs, forward)

    def f_done(p):
        f_copy(p, 0).wait()
        each(zs, lambda step: f_copy(p, step).wait())

    scale = 1.0 / math.sqrt(HD)
    lane_head = iota((1, width), 1) // HD
    head_lanes = [ones_where(lane_head == h) for h in range(heads)]
    own = ones_where(iota((wide, width), 0) // length == iota((wide, width), 1) // HD)
    pair_lane = iota((1, 2 * HD), 1)
    left, right = ones_where(pair_lane < HD), ones_where(pair_lane >= HD)
    copies = ones_where(iota((2 * HD, width), 0) % HD == iota((2 * HD, width), 1) % HD)
    feature, flat_lane = iota((width, 2 * width), 0), iota((width, 2 * width), 1)
    to_flat = (feature // HD) * 2 * HD + feature % HD
    evens, odds = ones_where(flat_lane == to_flat), ones_where(flat_lane == to_flat + HD)
    live = iota((span, wide), 0) < length + types

    def places(c):
        return (
            pl.ds(pl.multiple_of(c * length, length), length),
            pl.ds(pl.multiple_of(c * PAD, PAD), PAD),
            pl.ds(pl.multiple_of(c * span, PAD), span),
            pl.ds(pl.multiple_of(c * wide, length), wide),
        )

    def diagonal(text):
        q = qs[text, :]
        return jnp.concatenate([q * lanes for lanes in head_lanes], axis=0)

    def compact(blocks):
        picked = blocks[(heads - 1) * length :]
        for h in range(heads - 2, -1, -1):
            picked = jnp.where(lane_head == h, blocks[h * length : (h + 1) * length], picked)
        return picked.astype(BF16)

    def value_side(c):
        text, extra, both, diag = places(c)
        k = jnp.concatenate([ks[text, :], kv[extra, :]], axis=0)
        g_rows = []
        for h in range(heads):
            block_g = g_ref[h, c]
            g_rows += [block_g * left, block_g * right]
        g_diag = jnp.dot(
            jnp.concatenate(g_rows, axis=0), copies, preferred_element_type=F32
        ).astype(BF16) * own
        g_all[diag, :] = g_diag
        scores = lax.dot_general(k, diagonal(text), ROWS_ROWS, preferred_element_type=F32) * scale
        scores = jnp.where(live, scores, -jnp.inf)
        grown = jnp.exp(scores - jnp.max(scores, axis=0, keepdims=True))
        probs = grown * (1.0 / jnp.sum(grown, axis=0, keepdims=True))
        probs_all[both, :] = probs
        dv_all = jnp.dot(probs.astype(BF16), g_diag, preferred_element_type=F32).astype(BF16)
        dv[text, :], dvv[extra, :] = dv_all[:length], dv_all[length:]

    def key_side(c):
        text, extra, both, diag = places(c)
        v = jnp.concatenate([vs[text, :], vv[extra, :]], axis=0)
        probs = probs_all[both, :]
        prob_grads = lax.dot_general(v, g_all[diag, :], ROWS_ROWS, preferred_element_type=F32)
        dots = jnp.sum(prob_grads * probs, axis=0, keepdims=True)
        low = (probs * (prob_grads - dots) * scale).astype(BF16)
        lows[both, :] = low
        dk_all = jnp.dot(low, diagonal(text), preferred_element_type=F32).astype(BF16)
        dk[text, :], dkv[extra, :] = dk_all[:length], dk_all[length:]

    def query_side(c):
        text, extra, both, _ = places(c)
        k = jnp.concatenate([ks[text, :], kv[extra, :]], axis=0)
        dq[text, :] = compact(
            lax.dot_general(lows[both, :], k, COLS_COLS, preferred_element_type=F32)
        )

    def contexts(start, stop):
        def some(i, carry):
            even, odd = [], []
            for j in range(UNROLL):
                text, extra, both, _ = places(i * UNROLL + j)
                v = jnp.concatenate([vs[text, :], vv[extra, :]], axis=0)
                out = compact(lax.dot_general(
                    probs_all[both, :].astype(BF16), v, COLS_COLS, preferred_element_type=F32
                ))
                even.append(out[:half])
                odd.append(out[half:])
            flat = jnp.dot(
                jnp.concatenate(even, axis=0), evens, preferred_element_type=F32
            ) + jnp.dot(jnp.concatenate(odd, axis=0), odds, preferred_element_type=F32)
            flat = flat.astype(BF16)
            for j in range(UNROLL):
                for h in range(heads):
                    ctx_ref[h, i * UNROLL + j] = flat[
                        j * half : (j + 1) * half, h * 2 * HD : (h + 1) * 2 * HD
                    ]
            return carry

        lax.fori_loop(start * centres // (4 * UNROLL), stop * centres // (4 * UNROLL), some, 0)

    def over_centres(action, start, stop):
        def several(i, carry):
            for j in range(UNROLL):
                action(i * UNROLL + j)
            return carry

        lax.fori_loop(start * centres // (4 * UNROLL), stop * centres // (4 * UNROLL), several, 0)

    def weight_part(grads, extra):
        part = lax.dot_general(grads[...], tok[...], COLS_COLS, preferred_element_type=F32)
        if extra is not None:
            part += lax.dot_general(extra[...], vpad[...], COLS_COLS, preferred_element_type=F32)
        return part

    over_centres(value_side, 0, 4)
    part_ready(2, weight_part(dv, dvv))
    over_centres(key_side, 0, 2)
    x_done(2)
    over_centres(key_side, 2, 4)
    part_ready(1, weight_part(dk, dkv))
    few_k = lax.dot_general(spread, dkv[...], COLS_COLS, preferred_element_type=F32).astype(BF16)
    few_v = lax.dot_general(spread, dvv[...], COLS_COLS, preferred_element_type=F32).astype(BF16)
    vg = jnp.dot(few_k, wk_ref[...], preferred_element_type=F32) + jnp.dot(
        few_v, wv_ref[...], preferred_element_type=F32
    )
    for i in range(m):
        vg_out[i] = vg[:, i * share : (i + 1) * share]

    def vg_copy(step):
        peer = lax.rem(my + step, m)
        return send(vg_out.at[peer], vg_in.at[my], vg_sems, (step,), "mp", peer)

    def sh_copy(step):
        held = shared.at[me]
        return send(held, held, sh_sems, (step,), "nodes", lax.rem(me + step, n))

    each(m, lambda step: vg_copy(step).start())
    vg_in[pl.ds(my, 1)] = vg_out[pl.ds(my, 1)]
    over_centres(query_side, 0, 4)
    z_done(2)
    part_ready(0, weight_part(dq, None))
    each(m, lambda step: vg_copy(step).wait())
    total = vg_in[0]
    for i in range(1, m):
        total = total + vg_in[i]
    shared[pl.ds(me, 1)] = (total / count_col).astype(BF16)[None]
    each(n, lambda step: sh_copy(step).start())
    x_done(1)
    contexts(0, 1)
    x_done(0)
    a_done(2)
    z_done(1)
    contexts(1, 2)
    z_done(0)
    a_done(1)
    contexts(2, 3)
    each(n, lambda step: sh_copy(step).wait())
    shared_ref[...] = shared[...]
    a_done(0)
    contexts(3, 4)
    for p in (2, 1, 0):
        f_done(p)
    weights_ref[...] = w_all[...]


def layer(n, m, types, tokens, w_query, w_key, w_value, grads, owned_cls, send_rows, slots, counts):
    heads, centres, half, _ = grads.shape
    count, model = tokens.shape
    width = heads * HD
    pairs, slot_width, rows = centres * types, slots.shape[2], owned_cls.shape[1]
    share = owned_cls.shape[0]
    vmem = pl.BlockSpec(memory_space=pltpu.VMEM)
    extra = centres * PAD
    zs = n // 2
    chunk = -(-(width * (model // LANES)) // (n * 16)) * 16
    narrow, small = pltpu.VMEM((count, width), BF16), pltpu.VMEM((extra, width), BF16)
    near = pltpu.VMEM((3, zs, chunk, LANES), BF16)
    all_parts = (3, 2, zs, chunk, LANES)
    dma = pltpu.SemaphoreType.DMA
    return pl.pallas_call(
        functools.partial(layer_kernel, n, m, types),
        out_shape=(
            jax.ShapeDtypeStruct(grads.shape, BF16),
            jax.ShapeDtypeStruct(all_parts, BF16),
            jax.ShapeDtypeStruct((n, pairs, share), BF16),
            jax.ShapeDtypeStruct((zs, rows, 2 * pairs), BF16),
        ),
        in_specs=[vmem] * 9,
        out_specs=(vmem,) * 4,
        scratch_shapes=[
            pltpu.VMEM((slot_width, pairs), F32),
            pltpu.VMEM((n, slot_width, pairs), F32),
            pltpu.VMEM((n, pairs, share), F32),
            pltpu.VMEM((n, pairs, share), F32),
            pltpu.VMEM((m, pairs, share), BF16),
            pltpu.VMEM((count, model), BF16), pltpu.VMEM((extra, model), BF16),
            narrow, narrow, narrow, small, small, narrow, narrow, narrow, small, small,
            pltpu.VMEM((count + extra, width), BF16), pltpu.VMEM((count + extra, width), F32),
            pltpu.VMEM((count * heads, width), BF16),
            pltpu.VMEM(all_parts, BF16), near, near, near, pltpu.VMEM(all_parts, BF16),
            pltpu.VMEM((m, pairs, share), F32), pltpu.VMEM((m, pairs, share), F32),
            pltpu.VMEM((n, pairs, share), BF16),
            dma((2, n)), dma((2, n)), dma((2, m)), dma((2, m)), dma((2, n)),
            dma((2, 3)), dma((2, 3, zs)), dma((2, 3, zs)), dma((2, 3, zs)),
        ],
        compiler_params=pltpu.CompilerParams(
            collective_id=1, has_side_effects=True, vmem_limit_bytes=VMEM_LIMIT + n // 16 * 3 * 2**19
        ),
        name="layer",
    )(tokens, w_query, w_key, w_value, grads, owned_cls, send_rows, slots, counts)


STEPS = 2


def finish_kernel(weights_ref, shared_ref, mix_ref, q_ref, k_ref, v_ref, cls_ref):
    width, model = q_ref.shape
    groups = mix_ref.shape[0]
    for p, out in enumerate((q_ref, k_ref, v_ref)):
        for i in range(model // LANES):
            out[:, i * LANES : (i + 1) * LANES] = weights_ref[
                p, i * width : (i + 1) * width, :
            ].astype(F32)

    def product(g):
        both = jnp.concatenate([shared_ref[2 * g], shared_ref[2 * g + 1]], axis=0)
        turned = both.astype(F32).T.astype(BF16)
        return lax.dot_general(turned, mix_ref[g], ROWS_ROWS, preferred_element_type=F32)

    cls_ref[...] = product(0)

    def group(g, carry):
        cls_ref[...] += product(g)
        return carry

    lax.fori_loop(1, groups, group, 0)


def finish(weights, shared, mix, width, model):
    weight = jax.ShapeDtypeStruct((width, model), F32)
    groups, rows, lanes = mix.shape
    share = shared.shape[2]
    part = width * model // LANES // STEPS
    weight_spec = pl.BlockSpec((width, model // STEPS), lambda i: (0, i))
    return pl.pallas_call(
        finish_kernel,
        grid=(STEPS,),
        out_shape=(weight, weight, weight, jax.ShapeDtypeStruct((share, rows), F32)),
        in_specs=[
            pl.BlockSpec((3, part, LANES), lambda i: (0, i, 0)),
            pl.BlockSpec(shared.shape, lambda i: (0, 0, 0)),
            pl.BlockSpec((groups, rows // STEPS, lanes), lambda i: (0, i, 0)),
        ],
        out_specs=(weight_spec, weight_spec, weight_spec,
                   pl.BlockSpec((share, rows // STEPS), lambda i: (0, i))),
        compiler_params=pltpu.CompilerParams(vmem_limit_bytes=VMEM_LIMIT),
        name="finish",
    )(weights, shared, mix)


def body(n, m, tokens, w_query, w_key, w_value, grad_out, owned_cls, send_rows, neigh_slot, neigh_count):
    centres, length, model = tokens.shape
    width = w_query.shape[0]
    heads = width // HD
    grads = grad_out.transpose(1, 0, 2).reshape(heads, centres, length // 2, 2 * HD)
    context, weights, shared, mix = layer(
        n, m, neigh_slot.shape[1], tokens.reshape(-1, model), w_query, w_key, w_value, grads,
        owned_cls, send_rows[0], neigh_slot, neigh_count.T,
    )
    grad_q, grad_k, grad_v, grad_cls = finish(
        weights.reshape(3, -1, LANES), shared, mix, width, model
    )
    context = context.reshape(heads, centres, length * HD).transpose(1, 0, 2)
    return context, grad_q, grad_k, grad_v, grad_cls


def solution(mesh):
    in_specs = (
        P("nodes", None, None),
        P("mp", None),
        P("mp", None),
        P("mp", None),
        P("nodes", "mp", None),
        P("mp", "nodes"),
        P("nodes", None, None),
        P("nodes", None, None),
        P("nodes", None),
    )
    out_specs = (
        P("nodes", "mp", None),
        P("mp", None),
        P("mp", None),
        P("mp", None),
        P("mp", "nodes"),
    )
    return jax.shard_map(
        functools.partial(body, mesh.shape["nodes"], mesh.shape["mp"]),
        mesh=mesh, in_specs=in_specs, out_specs=out_specs, check_vma=False,
    )
```

```python
import functools
import math

import jax
import jax.numpy as jnp
from jax import lax
from jax.experimental import pallas as pl
from jax.experimental.pallas import tpu as pltpu
from jax.sharding import PartitionSpec as P

HD = 64
PAD = 16
LANES = 128
F32 = jnp.float32
BF16 = jnp.bfloat16
MESH = pl.DeviceIdType.MESH
VMEM_LIMIT = 56 * 1024 * 1024
ROWS_ROWS = (((1,), (1,)), ((), ()))
COLS_COLS = (((0,), (0,)), ((), ()))


def iota(shape, dim):
    return lax.broadcasted_iota(jnp.int32, shape, dim)


def ones_where(condition):
    return jnp.where(condition, 1.0, 0.0).astype(BF16)


def send(src, dst, sems, slot, axis, peer):
    return pltpu.make_async_remote_copy(
        src_ref=src,
        dst_ref=dst,
        send_sem=sems.at[(0, *slot)],
        recv_sem=sems.at[(1, *slot)],
        device_id={axis: peer},
        device_id_type=MESH,
    )


def greet(n, m, me, my):
    barrier = pltpu.get_barrier_semaphore()

    def hail(axis, size, here):
        def one(step, carry):
            pl.semaphore_signal(
                barrier, inc=1, device_id={axis: lax.rem(here + step, size)}, device_id_type=MESH
            )
            return carry

        lax.fori_loop(1, size, one, 0)

    hail("nodes", n, me)
    hail("mp", m, my)
    pl.semaphore_wait(barrier, n + m - 2)


def each(size, action):
    def one(step, carry):
        action(step)
        return carry

    lax.fori_loop(1, size, one, 0)


UNROLL = 4


def layer_kernel(
    n, m, types,
    tok_ref, wq_ref, wk_ref, wv_ref, g_ref, cls_ref, send_ref, slot_ref, count_ref,
    ctx_ref, weights_ref, shared_ref, mix_ref,
    slots_own, slots, parts, arrived, cols,
    tok, vpad, qs, ks, vs, kv, vv, dk, dv, dkv, dvv, probs_all, g_all,
    wsum, x_in, z_sum, z_in, w_all, vg_out, vg_in, shared,
    slot_sems, part_sems, col_sems, vg_sems, sh_sems, x_sems, z_sems, a_sems, f_sems,
):
    me, my = lax.axis_index("nodes"), lax.axis_index("mp")
    zs = n // 2
    par, zz = lax.rem(me, 2), lax.div(me, 2)
    mate = me + 1 - 2 * par
    rows = cls_ref.shape[1]
    cap = send_ref.shape[1]
    centres, _, slot_width = slot_ref.shape
    pairs = centres * types
    heads, _, half, _ = g_ref.shape
    length = 2 * half
    width = heads * HD
    model = tok_ref.shape[1]
    share = model // m
    span = length + PAD
    wide = heads * length

    counts = count_ref[...].astype(F32)
    lists = []
    for t in range(types):
        turned = slot_ref[:, t, :].astype(F32).T
        spot = iota((slot_width, centres), 0).astype(F32)
        lists.append(jnp.where(spot < counts[t : t + 1, :], turned, -1.0))
    slots_own[...] = jnp.concatenate(lists, axis=1)
    count_row = jnp.concatenate([counts[t : t + 1, :] for t in range(types)], axis=1)
    count_col = jnp.broadcast_to(count_row, (8, pairs)).T[:, :1]

    greet(n, m, me, my)

    def slot_copy(step):
        return send(slots_own, slots.at[me], slot_sems, (step,), "nodes", lax.rem(me + step, n))

    each(n, lambda step: slot_copy(step).start())
    slots[pl.ds(me, 1)] = slots_own[...][None]

    block = 4 * length
    to_row, from_row = iota((block, block), 0), iota((block, block), 1)
    inside = to_row % length
    swap = ones_where(
        from_row == (to_row - inside) + jnp.where(inside < half, 2 * inside, 2 * (inside - half) + 1)
    )

    def project(i, carry):
        here = pl.ds(pl.multiple_of(i * block, block), block)
        moved = jnp.dot(swap, tok_ref[here, :], preferred_element_type=F32).astype(BF16)
        tok[here, :] = moved
        for w_ref, out in ((wq_ref, qs), (wk_ref, ks), (wv_ref, vs)):
            out[here, :] = lax.dot_general(
                moved, w_ref[...], ROWS_ROWS, preferred_element_type=F32
            ).astype(BF16)
        return carry

    blocks = centres * length // block
    lax.fori_loop(0, blocks // 2, project, 0)
    each(n, lambda step: slot_copy(step).wait())

    chunk = 256
    lane = iota((cap, 2 * pairs), 1)
    target = (iota((cap, 2 * pairs), 0) + me * cap).astype(F32)

    def group(g, carry):
        wanted = jnp.concatenate([slots[2 * g], slots[2 * g + 1]], axis=1)
        total = jnp.zeros((cap, 2 * pairs), F32)
        for k in range(slot_width):
            total = total + jnp.where(target == wanted[k : k + 1, :], 1.0, 0.0)
        mixed = jnp.concatenate(
            [jnp.where(lane < pairs, total, 0.0), jnp.where(lane >= pairs, total, 0.0)], axis=0
        ).astype(BF16)
        chosen = jnp.concatenate(
            [send_ref[pl.ds(2 * g, 1), :], send_ref[pl.ds(2 * g + 1, 1), :]], axis=1
        )
        for r in range(0, rows, chunk):
            hot = ones_where(iota((chunk, 2 * cap), 0) + r == chosen)
            mix_ref[g, r : r + chunk, :] = jnp.dot(
                hot, mixed, preferred_element_type=F32
            ).astype(BF16)
        turned = jnp.dot(cls_ref[...], mix_ref[g], preferred_element_type=F32).T
        parts[2 * g] = turned[:pairs]
        parts[2 * g + 1] = turned[pairs:]
        return carry

    lax.fori_loop(0, n // 2, group, 0)

    def part_copy(step):
        peer = lax.rem(me + step, n)
        return send(parts.at[peer], arrived.at[me], part_sems, (step,), "nodes", peer)

    each(n, lambda step: part_copy(step).start())
    arrived[pl.ds(me, 1)] = parts[pl.ds(me, 1)]
    lax.fori_loop(blocks // 2, blocks, project, 0)
    each(n, lambda step: part_copy(step).wait())
    total = arrived[0]
    for b in range(1, n):
        total = total + arrived[b]
    cols[pl.ds(my, 1)] = (total / count_col).astype(BF16)[None]

    def col_copy(step):
        return send(cols.at[my], cols.at[my], col_sems, (step,), "mp", lax.rem(my + step, m))

    each(m, lambda step: col_copy(step).start())
    spread_row = iota((centres * PAD, pairs), 0)
    spread = ones_where(
        ((spread_row % PAD) * centres + spread_row // PAD == iota((centres * PAD, pairs), 1))
        & (spread_row % PAD < types)
    )
    each(m, lambda step: col_copy(step).wait())
    virt = jnp.concatenate([cols[i].astype(F32) for i in range(m)], axis=1).astype(BF16)
    vpad[...] = jnp.dot(spread, virt, preferred_element_type=F32).astype(BF16)
    kv[...] = lax.dot_general(
        vpad[...], wk_ref[...], ROWS_ROWS, preferred_element_type=F32
    ).astype(BF16)
    vv[...] = lax.dot_general(
        vpad[...], wv_ref[...], ROWS_ROWS, preferred_element_type=F32
    ).astype(BF16)

    units = model // LANES // 2
    value_part, key_part = (0, 2 * units, units), (1, units, units)
    query_parts = [(2 + i, i, 1) for i in range(units)]

    def x_copy(part):
        slot, at, size = part
        some = pl.ds(at, size)
        return send(wsum.at[1 - par, some], x_in.at[some], x_sems, (slot,), "nodes", mate)

    def z_copy(part, step):
        slot, at, size = part
        some = pl.ds(at, size)
        peer = lax.rem(zz + step, zs)
        return send(
            z_sum.at[some, peer], z_in.at[some, zz], z_sems, (slot, step), "nodes", 2 * peer + par
        )

    def a_copy(part, step):
        slot, at, size = part
        held = w_all.at[par, pl.ds(at, size), zz]
        return send(held, held, a_sems, (slot, step), "nodes", 2 * lax.rem(zz + step, zs) + par)

    def f_copy(part, step):
        slot, at, size = part
        held = w_all.at[par, pl.ds(at, size), lax.rem(zz - step + zs, zs)]
        return send(held, held, f_sems, (slot, step), "nodes", mate)

    def ready(parts_of, at, grads, extra):
        size = wsum.shape[2:]
        for side in (1 - par, par):
            lanes = pl.ds(pl.multiple_of(side * units * LANES, LANES), units * LANES)
            part = lax.dot_general(
                grads[...], tok[:, lanes], COLS_COLS, preferred_element_type=F32
            )
            if extra is not None:
                part += lax.dot_general(
                    extra[...], vpad[:, lanes], COLS_COLS, preferred_element_type=F32
                )
            for j in range(units):
                flat = part[:, j * LANES : (j + 1) * LANES].astype(BF16)
                short = size[0] * size[1] - width
                if short:
                    flat = jnp.concatenate([flat, jnp.zeros((short, LANES), BF16)], axis=0)
                wsum[side, at + j] = flat.reshape(size)
            if side is not par:
                for one in parts_of:
                    x_copy(one).start()

    def x_done(part):
        x_copy(part).wait()
        some = pl.ds(part[1], part[2])
        z_sum[some] = (wsum[par, some].astype(F32) + x_in[some].astype(F32)).astype(BF16)
        each(zs, lambda step: z_copy(part, step).start())
        z_in[some, pl.ds(zz, 1)] = z_sum[some, pl.ds(zz, 1)]

    def z_done(part):
        each(zs, lambda step: z_copy(part, step).wait())
        some = pl.ds(part[1], part[2])
        weights = z_in[some, 0].astype(F32)
        for b in range(1, zs):
            weights = weights + z_in[some, b].astype(F32)
        w_all[par, some, zz] = weights.astype(BF16)
        each(zs, lambda step: a_copy(part, step).start())
        f_copy(part, 0).start()

    def a_done(part):
        def forward(step):
            a_copy(part, step).wait()
            f_copy(part, step).start()

        each(zs, forward)

    def f_done(part):
        f_copy(part, 0).wait()
        each(zs, lambda step: f_copy(part, step).wait())

    scale = 1.0 / math.sqrt(HD)
    lane_head = iota((1, width), 1) // HD
    head_lanes = [ones_where(lane_head == h) for h in range(heads)]
    own = ones_where(iota((wide, width), 0) // length == iota((wide, width), 1) // HD)
    pair_lane = iota((1, 2 * HD), 1)
    left, right = ones_where(pair_lane < HD), ones_where(pair_lane >= HD)
    copies = ones_where(iota((2 * HD, width), 0) % HD == iota((2 * HD, width), 1) % HD)
    feature, flat_lane = iota((width, 2 * width), 0), iota((width, 2 * width), 1)
    to_flat = (feature // HD) * 2 * HD + feature % HD
    evens, odds = ones_where(flat_lane == to_flat), ones_where(flat_lane == to_flat + HD)
    live = iota((span, wide), 0) < length + types

    def places(c):
        return (
            pl.ds(pl.multiple_of(c * length, length), length),
            pl.ds(pl.multiple_of(c * PAD, PAD), PAD),
            pl.ds(pl.multiple_of(c * span, PAD), span),
            pl.ds(pl.multiple_of(c * wide, length), wide),
        )

    def kept(c):
        return pl.ds(pl.multiple_of(c * wide, length), span)

    def diagonal(text):
        q = qs[text, :]
        return jnp.concatenate([q * lanes for lanes in head_lanes], axis=0)

    def compact(blocks):
        picked = blocks[(heads - 1) * length :]
        for h in range(heads - 2, -1, -1):
            picked = jnp.where(lane_head == h, blocks[h * length : (h + 1) * length], picked)
        return picked.astype(BF16)

    def value_side(c):
        text, extra, both, diag = places(c)
        k = jnp.concatenate([ks[text, :], kv[extra, :]], axis=0)
        g_rows = []
        for h in range(heads):
            block_g = g_ref[h, c]
            g_rows += [block_g * left, block_g * right]
        g_diag = jnp.dot(
            jnp.concatenate(g_rows, axis=0), copies, preferred_element_type=F32
        ).astype(BF16) * own
        g_all[diag, :] = g_diag
        scores = lax.dot_general(k, diagonal(text), ROWS_ROWS, preferred_element_type=F32) * scale
        scores = jnp.where(live, scores, -jnp.inf)
        grown = jnp.exp(scores - jnp.max(scores, axis=0, keepdims=True))
        probs = grown * (1.0 / jnp.sum(grown, axis=0, keepdims=True))
        probs_all[both, :] = probs
        dv_all = jnp.dot(probs.astype(BF16), g_diag, preferred_element_type=F32).astype(BF16)
        dv[text, :], dvv[extra, :] = dv_all[:length], dv_all[length:]

    def key_side(c):
        text, extra, both, diag = places(c)
        v = jnp.concatenate([vs[text, :], vv[extra, :]], axis=0)
        probs = probs_all[both, :]
        prob_grads = lax.dot_general(v, g_all[diag, :], ROWS_ROWS, preferred_element_type=F32)
        dots = jnp.sum(prob_grads * probs, axis=0, keepdims=True)
        low = (probs * (prob_grads - dots) * scale).astype(BF16)
        g_all[kept(c), :] = low
        dk_all = jnp.dot(low, diagonal(text), preferred_element_type=F32).astype(BF16)
        dk[text, :], dkv[extra, :] = dk_all[:length], dk_all[length:]

    def query_side(c):
        text, extra, _, _ = places(c)
        k = jnp.concatenate([ks[text, :], kv[extra, :]], axis=0)
        qs[text, :] = compact(
            lax.dot_general(g_all[kept(c), :], k, COLS_COLS, preferred_element_type=F32)
        )

    def contexts(start, stop):
        def some(i, carry):
            even, odd = [], []
            for j in range(UNROLL):
                text, extra, both, _ = places(i * UNROLL + j)
                v = jnp.concatenate([vs[text, :], vv[extra, :]], axis=0)
                out = compact(lax.dot_general(
                    probs_all[both, :].astype(BF16), v, COLS_COLS, preferred_element_type=F32
                ))
                even.append(out[:half])
                odd.append(out[half:])
            flat = jnp.dot(
                jnp.concatenate(even, axis=0), evens, preferred_element_type=F32
            ) + jnp.dot(jnp.concatenate(odd, axis=0), odds, preferred_element_type=F32)
            flat = flat.astype(BF16)
            for j in range(UNROLL):
                for h in range(heads):
                    ctx_ref[h, i * UNROLL + j] = flat[
                        j * half : (j + 1) * half, h * 2 * HD : (h + 1) * 2 * HD
                    ]
            return carry

        lax.fori_loop(start * centres // (4 * UNROLL), stop * centres // (4 * UNROLL), some, 0)

    def over_centres(action, start, stop):
        def several(i, carry):
            for j in range(UNROLL):
                action(i * UNROLL + j)
            return carry

        lax.fori_loop(start * centres // (4 * UNROLL), stop * centres // (4 * UNROLL), several, 0)

    over_centres(value_side, 0, 4)
    ready([value_part], 2 * units, dv, dvv)
    over_centres(key_side, 0, 2)
    x_done(value_part)
    over_centres(key_side, 2, 4)
    z_done(value_part)
    ready([key_part], units, dk, dkv)
    few_k = lax.dot_general(spread, dkv[...], COLS_COLS, preferred_element_type=F32).astype(BF16)
    few_v = lax.dot_general(spread, dvv[...], COLS_COLS, preferred_element_type=F32).astype(BF16)
    vg = jnp.dot(few_k, wk_ref[...], preferred_element_type=F32) + jnp.dot(
        few_v, wv_ref[...], preferred_element_type=F32
    )
    for i in range(m):
        vg_out[i] = vg[:, i * share : (i + 1) * share]

    def vg_copy(step):
        peer = lax.rem(my + step, m)
        return send(vg_out.at[peer], vg_in.at[my], vg_sems, (step,), "mp", peer)

    def sh_copy(step):
        held = shared.at[me]
        return send(held, held, sh_sems, (step,), "nodes", lax.rem(me + step, n))

    each(m, lambda step: vg_copy(step).start())
    vg_in[pl.ds(my, 1)] = vg_out[pl.ds(my, 1)]
    over_centres(query_side, 0, 4)
    a_done(value_part)
    x_done(key_part)
    ready(query_parts, 0, qs, None)
    each(m, lambda step: vg_copy(step).wait())
    total = vg_in[0]
    for i in range(1, m):
        total = total + vg_in[i]
    shared[pl.ds(me, 1)] = (total / count_col).astype(BF16)[None]
    each(n, lambda step: sh_copy(step).start())
    z_done(key_part)
    contexts(0, 1)
    for part in query_parts:
        x_done(part)
    a_done(key_part)
    contexts(1, 2)
    for part in query_parts:
        z_done(part)
    contexts(2, 3)
    for part in query_parts:
        a_done(part)
    each(n, lambda step: sh_copy(step).wait())
    shared_ref[...] = shared[...]
    contexts(3, 4)
    for part in [value_part, key_part] + query_parts:
        f_done(part)
    weights_ref[...] = w_all[...]


def layer(n, m, types, tokens, w_query, w_key, w_value, grads, owned_cls, send_rows, slots, counts):
    heads, centres, half, _ = grads.shape
    count, model = tokens.shape
    width = heads * HD
    pairs, slot_width, rows = centres * types, slots.shape[2], owned_cls.shape[1]
    share = owned_cls.shape[0]
    vmem = pl.BlockSpec(memory_space=pltpu.VMEM)
    extra = centres * PAD
    zs = n // 2
    chunk = -(-width // (zs * 16)) * 16
    units = 3 * (model // LANES // 2)
    slots_of = 2 + units // 3
    narrow, small = pltpu.VMEM((count, width), BF16), pltpu.VMEM((extra, width), BF16)
    near = pltpu.VMEM((units, zs, chunk, LANES), BF16)
    all_parts = (2, units, zs, chunk, LANES)
    dma = pltpu.SemaphoreType.DMA
    return pl.pallas_call(
        functools.partial(layer_kernel, n, m, types),
        out_shape=(
            jax.ShapeDtypeStruct(grads.shape, BF16),
            jax.ShapeDtypeStruct(all_parts, BF16),
            jax.ShapeDtypeStruct((n, pairs, share), BF16),
            jax.ShapeDtypeStruct((zs, rows, 2 * pairs), BF16),
        ),
        in_specs=[vmem] * 9,
        out_specs=(vmem,) * 4,
        scratch_shapes=[
            pltpu.VMEM((slot_width, pairs), F32),
            pltpu.VMEM((n, slot_width, pairs), F32),
            pltpu.VMEM((n, pairs, share), F32),
            pltpu.VMEM((n, pairs, share), F32),
            pltpu.VMEM((m, pairs, share), BF16),
            pltpu.VMEM((count, model), BF16), pltpu.VMEM((extra, model), BF16),
            narrow, narrow, narrow, small, small, narrow, narrow, small, small,
            pltpu.VMEM((count + extra, width), F32),
            pltpu.VMEM((count * heads, width), BF16),
            pltpu.VMEM(all_parts, BF16), near, near, near, pltpu.VMEM(all_parts, BF16),
            pltpu.VMEM((m, pairs, share), F32), pltpu.VMEM((m, pairs, share), F32),
            pltpu.VMEM((n, pairs, share), BF16),
            dma((2, n)), dma((2, n)), dma((2, m)), dma((2, m)), dma((2, n)),
            dma((2, slots_of)), dma((2, slots_of, zs)), dma((2, slots_of, zs)), dma((2, slots_of, zs)),
        ],
        compiler_params=pltpu.CompilerParams(
            collective_id=1, has_side_effects=True, vmem_limit_bytes=VMEM_LIMIT + n // 16 * 7 * 2**18
        ),
        name="layer",
    )(tokens, w_query, w_key, w_value, grads, owned_cls, send_rows, slots, counts)


STEPS = 2


def finish_kernel(weights_ref, shared_ref, mix_ref, q_ref, k_ref, v_ref, cls_ref):
    width, model = q_ref.shape
    groups = mix_ref.shape[0]
    for p, out in enumerate((q_ref, k_ref, v_ref)):
        units = model // LANES
        for i in range(units):
            out[:, i * LANES : (i + 1) * LANES] = weights_ref[0, p * units + i].astype(F32)

    def product(g):
        both = jnp.concatenate([shared_ref[2 * g], shared_ref[2 * g + 1]], axis=0)
        turned = both.astype(F32).T.astype(BF16)
        return lax.dot_general(turned, mix_ref[g], ROWS_ROWS, preferred_element_type=F32)

    cls_ref[...] = product(0)

    def group(g, carry):
        cls_ref[...] += product(g)
        return carry

    lax.fori_loop(1, groups, group, 0)


def finish(weights, shared, mix, width, model):
    weight = jax.ShapeDtypeStruct((width, model), F32)
    groups, rows, lanes = mix.shape
    share = shared.shape[2]
    weight_spec = pl.BlockSpec((width, model // STEPS), lambda i: (0, i))
    return pl.pallas_call(
        finish_kernel,
        grid=(STEPS,),
        out_shape=(weight, weight, weight, jax.ShapeDtypeStruct((share, rows), F32)),
        in_specs=[
            pl.BlockSpec((1, weights.shape[1], width, LANES), lambda i: (i, 0, 0, 0)),
            pl.BlockSpec(shared.shape, lambda i: (0, 0, 0)),
            pl.BlockSpec((groups, rows // STEPS, lanes), lambda i: (0, i, 0)),
        ],
        out_specs=(weight_spec, weight_spec, weight_spec,
                   pl.BlockSpec((share, rows // STEPS), lambda i: (0, i))),
        compiler_params=pltpu.CompilerParams(vmem_limit_bytes=VMEM_LIMIT),
        name="finish",
    )(weights, shared, mix)


def body(n, m, tokens, w_query, w_key, w_value, grad_out, owned_cls, send_rows, neigh_slot, neigh_count):
    centres, length, model = tokens.shape
    width = w_query.shape[0]
    heads = width // HD
    grads = grad_out.transpose(1, 0, 2).reshape(heads, centres, length // 2, 2 * HD)
    context, weights, shared, mix = layer(
        n, m, neigh_slot.shape[1], tokens.reshape(-1, model), w_query, w_key, w_value, grads,
        owned_cls, send_rows[0], neigh_slot, neigh_count.T,
    )
    grad_q, grad_k, grad_v, grad_cls = finish(
        weights.reshape(*weights.shape[:2], -1, LANES), shared, mix, width, model
    )
    context = context.reshape(heads, centres, length * HD).transpose(1, 0, 2)
    return context, grad_q, grad_k, grad_v, grad_cls


def solution(mesh):
    in_specs = (
        P("nodes", None, None),
        P("mp", None),
        P("mp", None),
        P("mp", None),
        P("nodes", "mp", None),
        P("mp", "nodes"),
        P("nodes", None, None),
        P("nodes", None, None),
        P("nodes", None),
    )
    out_specs = (
        P("nodes", "mp", None),
        P("mp", None),
        P("mp", None),
        P("mp", None),
        P("mp", "nodes"),
    )
    return jax.shard_map(
        functools.partial(body, mesh.shape["nodes"], mesh.shape["mp"]),
        mesh=mesh, in_specs=in_specs, out_specs=out_specs, check_vma=False,
    )
```

```python
import functools
import math

import jax
import jax.numpy as jnp
from jax import lax
from jax.experimental import pallas as pl
from jax.experimental.pallas import tpu as pltpu
from jax.sharding import PartitionSpec as P

HD = 64
PAD = 16
LANES = 128
F32 = jnp.float32
BF16 = jnp.bfloat16
MESH = pl.DeviceIdType.MESH
VMEM_LIMIT = 56 * 1024 * 1024
ROWS_ROWS = (((1,), (1,)), ((), ()))
COLS_COLS = (((0,), (0,)), ((), ()))


def iota(shape, dim):
    return lax.broadcasted_iota(jnp.int32, shape, dim)


def ones_where(condition):
    return jnp.where(condition, 1.0, 0.0).astype(BF16)


def send(src, dst, sems, slot, axis, peer):
    return pltpu.make_async_remote_copy(
        src_ref=src,
        dst_ref=dst,
        send_sem=sems.at[(0, *slot)],
        recv_sem=sems.at[(1, *slot)],
        device_id={axis: peer},
        device_id_type=MESH,
    )


def greet(n, m, me, my):
    barrier = pltpu.get_barrier_semaphore()

    def hail(axis, size, here):
        def one(step, carry):
            pl.semaphore_signal(
                barrier, inc=1, device_id={axis: lax.rem(here + step, size)}, device_id_type=MESH
            )
            return carry

        lax.fori_loop(1, size, one, 0)

    hail("nodes", n, me)
    hail("mp", m, my)
    pl.semaphore_wait(barrier, n + m - 2)


def each(size, action):
    def one(step, carry):
        action(step)
        return carry

    lax.fori_loop(1, size, one, 0)


UNROLL = 4


def layer_kernel(
    n, m, types,
    tok_ref, wq_ref, wk_ref, wv_ref, g_ref, cls_ref, send_ref, slot_ref, count_ref,
    ctx_ref, weights_ref, shared_ref, mix_ref,
    slots_own, slots, parts, arrived, cols,
    tok, vpad, qs, ks, vs, kv, vv, dk, dv, dkv, dvv, probs_all, g_all,
    wsum, x_in, z_sum, z_in, w_all, vg_out, vg_in, shared,
    slot_sems, part_sems, col_sems, vg_sems, sh_sems, x_sems, z_sems, a_sems, f_sems,
):
    me, my = lax.axis_index("nodes"), lax.axis_index("mp")
    zs = n // 2
    par, zz = lax.rem(me, 2), lax.div(me, 2)
    mate = me + 1 - 2 * par
    rows = cls_ref.shape[1]
    cap = send_ref.shape[1]
    centres, _, slot_width = slot_ref.shape
    pairs = centres * types
    heads, _, half, _ = g_ref.shape
    length = 2 * half
    width = heads * HD
    model = tok_ref.shape[1]
    share = model // m
    span = length + PAD
    wide = heads * length

    counts = count_ref[...].astype(F32)
    lists = []
    for t in range(types):
        turned = slot_ref[:, t, :].astype(F32).T
        spot = iota((slot_width, centres), 0).astype(F32)
        lists.append(jnp.where(spot < counts[t : t + 1, :], turned, -1.0))
    slots_own[...] = jnp.concatenate(lists, axis=1)
    count_row = jnp.concatenate([counts[t : t + 1, :] for t in range(types)], axis=1)
    count_col = jnp.broadcast_to(count_row, (8, pairs)).T[:, :1]

    greet(n, m, me, my)

    def slot_copy(step):
        return send(slots_own, slots.at[me], slot_sems, (step,), "nodes", lax.rem(me + step, n))

    each(n, lambda step: slot_copy(step).start())
    slots[pl.ds(me, 1)] = slots_own[...][None]

    block = 4 * length
    to_row, from_row = iota((block, block), 0), iota((block, block), 1)
    inside = to_row % length
    swap = ones_where(
        from_row == (to_row - inside) + jnp.where(inside < half, 2 * inside, 2 * (inside - half) + 1)
    )

    def project(i, carry):
        here = pl.ds(pl.multiple_of(i * block, block), block)
        moved = jnp.dot(swap, tok_ref[here, :], preferred_element_type=F32).astype(BF16)
        tok[here, :] = moved
        for w_ref, out in ((wq_ref, qs), (wk_ref, ks), (wv_ref, vs)):
            out[here, :] = lax.dot_general(
                moved, w_ref[...], ROWS_ROWS, preferred_element_type=F32
            ).astype(BF16)
        return carry

    blocks = centres * length // block
    lax.fori_loop(0, blocks // 2, project, 0)
    each(n, lambda step: slot_copy(step).wait())

    chunk = 256
    lane = iota((cap, 2 * pairs), 1)
    target = (iota((cap, 2 * pairs), 0) + me * cap).astype(F32)

    def part_copy(peer):
        step = lax.rem(peer - me + n, n)
        return send(parts.at[peer], arrived.at[me], part_sems, (step,), "nodes", peer)

    def group(i, carry):
        g = lax.rem(zz + 1 + i, zs)
        wanted = jnp.concatenate([slots[2 * g], slots[2 * g + 1]], axis=1)
        total = jnp.zeros((cap, 2 * pairs), F32)
        for k in range(slot_width):
            total = total + jnp.where(target == wanted[k : k + 1, :], 1.0, 0.0)
        mixed = jnp.concatenate(
            [jnp.where(lane < pairs, total, 0.0), jnp.where(lane >= pairs, total, 0.0)], axis=0
        ).astype(BF16)
        chosen = jnp.concatenate(
            [send_ref[pl.ds(2 * g, 1), :], send_ref[pl.ds(2 * g + 1, 1), :]], axis=1
        )
        for r in range(0, rows, chunk):
            hot = ones_where(iota((chunk, 2 * cap), 0) + r == chosen)
            mix_ref[g, r : r + chunk, :] = jnp.dot(
                hot, mixed, preferred_element_type=F32
            ).astype(BF16)
        turned = jnp.dot(cls_ref[...], mix_ref[g], preferred_element_type=F32).T
        turned = turned.astype(BF16)
        for side in range(2):
            peer = 2 * g + side
            parts[peer] = turned[side * pairs : (side + 1) * pairs]

            @pl.when(peer != me)
            def _():
                part_copy(peer).start()

        return carry

    lax.fori_loop(0, n // 2, group, 0)

    arrived[pl.ds(me, 1)] = parts[pl.ds(me, 1)]
    lax.fori_loop(blocks // 2, blocks, project, 0)
    each(n, lambda step: part_copy(lax.rem(me + step, n)).wait())
    total = arrived[0].astype(F32)
    for b in range(1, n):
        total = total + arrived[b].astype(F32)
    cols[pl.ds(my, 1)] = (total / count_col).astype(BF16)[None]

    def col_copy(step):
        return send(cols.at[my], cols.at[my], col_sems, (step,), "mp", lax.rem(my + step, m))

    each(m, lambda step: col_copy(step).start())
    spread_row = iota((centres * PAD, pairs), 0)
    spread = ones_where(
        ((spread_row % PAD) * centres + spread_row // PAD == iota((centres * PAD, pairs), 1))
        & (spread_row % PAD < types)
    )
    units = model // LANES // 2
    value_part, key_part = (0, 2 * units, units), (1, units, units)
    query_parts = [(2 + i, i, 1) for i in range(units)]

    def x_copy(part):
        slot, at, size = part
        some = pl.ds(at, size)
        return send(wsum.at[1 - par, some], x_in.at[some], x_sems, (slot,), "nodes", mate)

    def z_copy(part, step):
        slot, at, size = part
        some = pl.ds(at, size)
        peer = lax.rem(zz + step, zs)
        return send(
            z_sum.at[some, peer], z_in.at[some, zz], z_sems, (slot, step), "nodes", 2 * peer + par
        )

    def a_copy(part, step):
        slot, at, size = part
        held = w_all.at[par, pl.ds(at, size), zz]
        return send(held, held, a_sems, (slot, step), "nodes", 2 * lax.rem(zz + step, zs) + par)

    def f_copy(part, step):
        slot, at, size = part
        held = w_all.at[par, pl.ds(at, size), lax.rem(zz - step + zs, zs)]
        return send(held, held, f_sems, (slot, step), "nodes", mate)

    def ready(parts_of, at, grads, extra):
        size = wsum.shape[2:]
        for side in (1 - par, par):
            lanes = pl.ds(pl.multiple_of(side * units * LANES, LANES), units * LANES)
            part = lax.dot_general(
                grads[...], tok[:, lanes], COLS_COLS, preferred_element_type=F32
            )
            if extra is not None:
                part += lax.dot_general(
                    extra[...], vpad[:, lanes], COLS_COLS, preferred_element_type=F32
                )
            for j in range(units):
                flat = part[:, j * LANES : (j + 1) * LANES].astype(BF16)
                short = size[0] * size[1] - width
                if short:
                    flat = jnp.concatenate([flat, jnp.zeros((short, LANES), BF16)], axis=0)
                wsum[side, at + j] = flat.reshape(size)
            if side is not par:
                for one in parts_of:
                    x_copy(one).start()

    def x_done(part):
        x_copy(part).wait()
        some = pl.ds(part[1], part[2])
        z_sum[some] = (wsum[par, some].astype(F32) + x_in[some].astype(F32)).astype(BF16)
        each(zs, lambda step: z_copy(part, step).start())
        z_in[some, pl.ds(zz, 1)] = z_sum[some, pl.ds(zz, 1)]

    def z_done(part):
        each(zs, lambda step: z_copy(part, step).wait())
        some = pl.ds(part[1], part[2])
        weights = z_in[some, 0].astype(F32)
        for b in range(1, zs):
            weights = weights + z_in[some, b].astype(F32)
        w_all[par, some, zz] = weights.astype(BF16)
        each(zs, lambda step: a_copy(part, step).start())
        f_copy(part, 0).start()

    def a_done(part):
        def forward(step):
            a_copy(part, step).wait()
            f_copy(part, step).start()

        each(zs, forward)

    def f_done(part):
        f_copy(part, 0).wait()
        each(zs, lambda step: f_copy(part, step).wait())

    scale = 1.0 / math.sqrt(HD)
    lane_head = iota((1, width), 1) // HD
    head_lanes = [ones_where(lane_head == h) for h in range(heads)]
    own = ones_where(iota((wide, width), 0) // length == iota((wide, width), 1) // HD)
    pair_lane = iota((1, 2 * HD), 1)
    left, right = ones_where(pair_lane < HD), ones_where(pair_lane >= HD)
    copies = ones_where(iota((2 * HD, width), 0) % HD == iota((2 * HD, width), 1) % HD)
    feature, flat_lane = iota((width, 2 * width), 0), iota((width, 2 * width), 1)
    to_flat = (feature // HD) * 2 * HD + feature % HD
    evens, odds = ones_where(flat_lane == to_flat), ones_where(flat_lane == to_flat + HD)
    live = iota((span, wide), 0) < length + types

    def places(c):
        return (
            pl.ds(pl.multiple_of(c * length, length), length),
            pl.ds(pl.multiple_of(c * PAD, PAD), PAD),
            pl.ds(pl.multiple_of(c * span, PAD), span),
            pl.ds(pl.multiple_of(c * wide, length), wide),
        )

    def kept(c):
        return pl.ds(pl.multiple_of(c * wide, length), span)

    def diagonal(text):
        q = qs[text, :]
        return jnp.concatenate([q * lanes for lanes in head_lanes], axis=0)

    def compact(blocks):
        picked = blocks[(heads - 1) * length :]
        for h in range(heads - 2, -1, -1):
            picked = jnp.where(lane_head == h, blocks[h * length : (h + 1) * length], picked)
        return picked.astype(BF16)

    def lay_out(c):
        _, _, _, diag = places(c)
        g_rows = []
        for h in range(heads):
            block_g = g_ref[h, c]
            g_rows += [block_g * left, block_g * right]
        g_diag = jnp.dot(
            jnp.concatenate(g_rows, axis=0), copies, preferred_element_type=F32
        ).astype(BF16) * own
        g_all[diag, :] = g_diag

    def value_side(c):
        text, extra, both, diag = places(c)
        k = jnp.concatenate([ks[text, :], kv[extra, :]], axis=0)
        scores = lax.dot_general(k, diagonal(text), ROWS_ROWS, preferred_element_type=F32) * scale
        scores = jnp.where(live, scores, -jnp.inf)
        grown = jnp.exp(scores - jnp.max(scores, axis=0, keepdims=True))
        probs = grown * (1.0 / jnp.sum(grown, axis=0, keepdims=True))
        probs_all[both, :] = probs
        dv_all = jnp.dot(probs.astype(BF16), g_all[diag, :], preferred_element_type=F32).astype(BF16)
        dv[text, :], dvv[extra, :] = dv_all[:length], dv_all[length:]

    def key_side(c):
        text, extra, both, diag = places(c)
        v = jnp.concatenate([vs[text, :], vv[extra, :]], axis=0)
        probs = probs_all[both, :]
        prob_grads = lax.dot_general(v, g_all[diag, :], ROWS_ROWS, preferred_element_type=F32)
        dots = jnp.sum(prob_grads * probs, axis=0, keepdims=True)
        low = (probs * (prob_grads - dots) * scale).astype(BF16)
        g_all[kept(c), :] = low
        dk_all = jnp.dot(low, diagonal(text), preferred_element_type=F32).astype(BF16)
        dk[text, :], dkv[extra, :] = dk_all[:length], dk_all[length:]

    def query_side(c):
        text, extra, _, _ = places(c)
        k = jnp.concatenate([ks[text, :], kv[extra, :]], axis=0)
        qs[text, :] = compact(
            lax.dot_general(g_all[kept(c), :], k, COLS_COLS, preferred_element_type=F32)
        )

    def contexts(start, stop):
        def some(i, carry):
            even, odd = [], []
            for j in range(UNROLL):
                text, extra, both, _ = places(i * UNROLL + j)
                v = jnp.concatenate([vs[text, :], vv[extra, :]], axis=0)
                out = compact(lax.dot_general(
                    probs_all[both, :].astype(BF16), v, COLS_COLS, preferred_element_type=F32
                ))
                even.append(out[:half])
                odd.append(out[half:])
            flat = jnp.dot(
                jnp.concatenate(even, axis=0), evens, preferred_element_type=F32
            ) + jnp.dot(jnp.concatenate(odd, axis=0), odds, preferred_element_type=F32)
            flat = flat.astype(BF16)
            for j in range(UNROLL):
                for h in range(heads):
                    ctx_ref[h, i * UNROLL + j] = flat[
                        j * half : (j + 1) * half, h * 2 * HD : (h + 1) * 2 * HD
                    ]
            return carry

        lax.fori_loop(start * centres // (4 * UNROLL), stop * centres // (4 * UNROLL), some, 0)

    def over_centres(action, start, stop):
        def several(i, carry):
            for j in range(UNROLL):
                action(i * UNROLL + j)
            return carry

        lax.fori_loop(start * centres // (4 * UNROLL), stop * centres // (4 * UNROLL), several, 0)

    over_centres(lay_out, 0, 4)
    each(m, lambda step: col_copy(step).wait())
    virt = jnp.concatenate([cols[i].astype(F32) for i in range(m)], axis=1).astype(BF16)
    vpad[...] = jnp.dot(spread, virt, preferred_element_type=F32).astype(BF16)
    kv[...] = lax.dot_general(
        vpad[...], wk_ref[...], ROWS_ROWS, preferred_element_type=F32
    ).astype(BF16)
    vv[...] = lax.dot_general(
        vpad[...], wv_ref[...], ROWS_ROWS, preferred_element_type=F32
    ).astype(BF16)

    over_centres(value_side, 0, 4)
    ready([value_part], 2 * units, dv, dvv)
    over_centres(key_side, 0, 2)
    x_done(value_part)
    over_centres(key_side, 2, 4)
    z_done(value_part)
    ready([key_part], units, dk, dkv)
    few_k = lax.dot_general(spread, dkv[...], COLS_COLS, preferred_element_type=F32).astype(BF16)
    few_v = lax.dot_general(spread, dvv[...], COLS_COLS, preferred_element_type=F32).astype(BF16)
    vg = jnp.dot(few_k, wk_ref[...], preferred_element_type=F32) + jnp.dot(
        few_v, wv_ref[...], preferred_element_type=F32
    )
    for i in range(m):
        vg_out[i] = vg[:, i * share : (i + 1) * share]

    def vg_copy(step):
        peer = lax.rem(my + step, m)
        return send(vg_out.at[peer], vg_in.at[my], vg_sems, (step,), "mp", peer)

    def sh_copy(step):
        held = shared.at[me]
        peer = 2 * lax.rem(zz + step, zs) + par
        return send(held, held, sh_sems, (0, step), "nodes", peer)

    def sh_pass(step):
        held = shared.at[2 * lax.rem(zz - step + zs, zs) + par]
        return send(held, held, sh_sems, (1, step), "nodes", mate)

    def sh_forward(step):
        sh_copy(step).wait()
        sh_pass(step).start()

    each(m, lambda step: vg_copy(step).start())
    vg_in[pl.ds(my, 1)] = vg_out[pl.ds(my, 1)]
    over_centres(query_side, 0, 4)
    a_done(value_part)
    x_done(key_part)
    ready(query_parts, 0, qs, None)
    each(m, lambda step: vg_copy(step).wait())
    total = vg_in[0]
    for i in range(1, m):
        total = total + vg_in[i]
    shared[pl.ds(me, 1)] = (total / count_col).astype(BF16)[None]
    each(zs, lambda step: sh_copy(step).start())
    sh_pass(0).start()
    z_done(key_part)
    contexts(0, 1)
    for part in query_parts:
        x_done(part)
    a_done(key_part)
    each(zs, sh_forward)
    contexts(1, 2)
    for part in query_parts:
        z_done(part)
    contexts(2, 3)
    for part in query_parts:
        a_done(part)
    contexts(3, 4)
    sh_pass(0).wait()
    each(zs, lambda step: sh_pass(step).wait())
    shared_ref[...] = shared[...]
    for part in [value_part, key_part] + query_parts:
        f_done(part)
    weights_ref[...] = w_all[...]


def layer(n, m, types, tokens, w_query, w_key, w_value, grads, owned_cls, send_rows, slots, counts):
    heads, centres, half, _ = grads.shape
    count, model = tokens.shape
    width = heads * HD
    pairs, slot_width, rows = centres * types, slots.shape[2], owned_cls.shape[1]
    share = owned_cls.shape[0]
    vmem = pl.BlockSpec(memory_space=pltpu.VMEM)
    extra = centres * PAD
    zs = n // 2
    chunk = -(-width // (zs * 16)) * 16
    units = 3 * (model // LANES // 2)
    slots_of = 2 + units // 3
    narrow, small = pltpu.VMEM((count, width), BF16), pltpu.VMEM((extra, width), BF16)
    near = pltpu.VMEM((units, zs, chunk, LANES), BF16)
    all_parts = (2, units, zs, chunk, LANES)
    dma = pltpu.SemaphoreType.DMA
    return pl.pallas_call(
        functools.partial(layer_kernel, n, m, types),
        out_shape=(
            jax.ShapeDtypeStruct(grads.shape, BF16),
            jax.ShapeDtypeStruct(all_parts, BF16),
            jax.ShapeDtypeStruct((n, pairs, share), BF16),
            jax.ShapeDtypeStruct((zs, rows, 2 * pairs), BF16),
        ),
        in_specs=[vmem] * 9,
        out_specs=(vmem,) * 4,
        scratch_shapes=[
            pltpu.VMEM((slot_width, pairs), F32),
            pltpu.VMEM((n, slot_width, pairs), F32),
            pltpu.VMEM((n, pairs, share), BF16),
            pltpu.VMEM((n, pairs, share), BF16),
            pltpu.VMEM((m, pairs, share), BF16),
            pltpu.VMEM((count, model), BF16), pltpu.VMEM((extra, model), BF16),
            narrow, narrow, narrow, small, small, narrow, narrow, small, small,
            pltpu.VMEM((count + extra, width), F32),
            pltpu.VMEM((count * heads, width), BF16),
            pltpu.VMEM(all_parts, BF16), near, near, near, pltpu.VMEM(all_parts, BF16),
            pltpu.VMEM((m, pairs, share), F32), pltpu.VMEM((m, pairs, share), F32),
            pltpu.VMEM((n, pairs, share), BF16),
            dma((2, n)), dma((2, n)), dma((2, m)), dma((2, m)), dma((2, 2, zs)),
            dma((2, slots_of)), dma((2, slots_of, zs)), dma((2, slots_of, zs)), dma((2, slots_of, zs)),
        ],
        compiler_params=pltpu.CompilerParams(
            collective_id=1, has_side_effects=True, vmem_limit_bytes=VMEM_LIMIT + n // 16 * 7 * 2**18
        ),
        name="layer",
    )(tokens, w_query, w_key, w_value, grads, owned_cls, send_rows, slots, counts)


STEPS = 2


def finish_kernel(weights_ref, shared_ref, mix_ref, q_ref, k_ref, v_ref, cls_ref):
    width, model = q_ref.shape
    groups = mix_ref.shape[0]
    for p, out in enumerate((q_ref, k_ref, v_ref)):
        units = model // LANES
        for i in range(units):
            out[:, i * LANES : (i + 1) * LANES] = weights_ref[0, p * units + i].astype(F32)

    def product(g):
        both = jnp.concatenate([shared_ref[2 * g], shared_ref[2 * g + 1]], axis=0)
        turned = both.astype(F32).T.astype(BF16)
        return lax.dot_general(turned, mix_ref[g], ROWS_ROWS, preferred_element_type=F32)

    cls_ref[...] = product(0)

    def group(g, carry):
        cls_ref[...] += product(g)
        return carry

    lax.fori_loop(1, groups, group, 0)


def finish(weights, shared, mix, width, model):
    weight = jax.ShapeDtypeStruct((width, model), F32)
    groups, rows, lanes = mix.shape
    share = shared.shape[2]
    weight_spec = pl.BlockSpec((width, model // STEPS), lambda i: (0, i))
    return pl.pallas_call(
        finish_kernel,
        grid=(STEPS,),
        out_shape=(weight, weight, weight, jax.ShapeDtypeStruct((share, rows), F32)),
        in_specs=[
            pl.BlockSpec((1, weights.shape[1], width, LANES), lambda i: (i, 0, 0, 0)),
            pl.BlockSpec(shared.shape, lambda i: (0, 0, 0)),
            pl.BlockSpec((groups, rows // STEPS, lanes), lambda i: (0, i, 0)),
        ],
        out_specs=(weight_spec, weight_spec, weight_spec,
                   pl.BlockSpec((share, rows // STEPS), lambda i: (0, i))),
        compiler_params=pltpu.CompilerParams(vmem_limit_bytes=VMEM_LIMIT),
        name="finish",
    )(weights, shared, mix)


def body(n, m, tokens, w_query, w_key, w_value, grad_out, owned_cls, send_rows, neigh_slot, neigh_count):
    centres, length, model = tokens.shape
    width = w_query.shape[0]
    heads = width // HD
    grads = grad_out.transpose(1, 0, 2).reshape(heads, centres, length // 2, 2 * HD)
    context, weights, shared, mix = layer(
        n, m, neigh_slot.shape[1], tokens.reshape(-1, model), w_query, w_key, w_value, grads,
        owned_cls, send_rows[0], neigh_slot, neigh_count.T,
    )
    grad_q, grad_k, grad_v, grad_cls = finish(
        weights.reshape(*weights.shape[:2], -1, LANES), shared, mix, width, model
    )
    context = context.reshape(heads, centres, length * HD).transpose(1, 0, 2)
    return context, grad_q, grad_k, grad_v, grad_cls


def solution(mesh):
    in_specs = (
        P("nodes", None, None),
        P("mp", None),
        P("mp", None),
        P("mp", None),
        P("nodes", "mp", None),
        P("mp", "nodes"),
        P("nodes", None, None),
        P("nodes", None, None),
        P("nodes", None),
    )
    out_specs = (
        P("nodes", "mp", None),
        P("mp", None),
        P("mp", None),
        P("mp", None),
        P("mp", "nodes"),
    )
    return jax.shard_map(
        functools.partial(body, mesh.shape["nodes"], mesh.shape["mp"]),
        mesh=mesh, in_specs=in_specs, out_specs=out_specs, check_vma=False,
    )
```
